256 devices in a mesh: visit: 16 (over z, core), patch: 16 (over y, x).
Axes of the slice: x: 4, y: 4, z: 8, core: 2. Of those that a mesh axis runs over, the one named last changes fastest.
Arguments:
- images: bfloat16 [16, 4096, 4096], P('visit', 'patch'), may hold values from -6 to 6
- psf_taps: bfloat16 [16, 2, 13], P('visit'), may hold values from 0.019897461 to 0.19921875
- exposure_weights: float32 [16], P('visit'), may hold values from 0.5 to 8
- dest_patch: int32 [16, 32, 32], P('visit', 'patch'), may hold values from -1 to 15, as said below
- dest_cell: int32 [16, 32, 32], P('visit', 'patch'), may hold values from -1 to 63, as said below
- shift_class: int32 [16, 2, 32, 32], P('visit', None, 'patch'), may hold values from 0 to 7
Outputs:
- coadd: float32 [16, 64, 128, 128], P('patch', 'visit')
- weight_map: float32 [16, 64], P('patch', 'visit')
The draws below stay inside these ranges and needn't reach their ends.
Inputs may be any that keep to these rules, and one draw needn't show every extreme that they name: `dest_patch`: within one exposure all tiles move to sky cells by one whole-cell offset of at most 2 cells along each direction, so distinct tiles land in distinct cells; the patch of cell row u and column w is (u // 8) * 4 + w // 8. Of the 64 tiles in one exposure's band of 256 rows, at most 16 fall in any one patch. `dest_cell`: cell index (u % 8) * 8 + w % 8; -1 exactly where dest_patch is -1.
All inputs are finite; a program needn't handle non-finite values.
Results may differ from the reference program's by a relative error of at most 0.0004.
The reference program's roundings to bfloat16 on the way count: a program that leaves them out, or rounds other values in their place, can miss the bound.
Values may be sent and summed in bfloat16 or wider, within the bound.
No kernel may reach another device: no remote copies, remote signals or barrier semaphores. Data moves between devices by JAX's collectives and lax.ppermute only.
A program may use at most 128 MiB of HBM per device.

```python
import math
import jax
import jax.numpy as jnp
from jax import lax

TILE = 128
KTAPS = 13
SHIFTS = 8
PCELLS = 8
COLS = 4096
ROWS = 4096
EXPOS = 16
PATCHES = 16
CELLS = 64


def sky_cells(key):
    reach = 2
    shift_y = jax.random.randint(jax.random.fold_in(key, 11), (EXPOS, 1, 1), -reach, reach + 1)
    shift_x = jax.random.randint(jax.random.fold_in(key, 12), (EXPOS, 1, 1), -reach, reach + 1)
    grid_rows = ROWS // TILE
    grid_cols = COLS // TILE
    cell_y = jnp.arange(grid_rows, dtype=jnp.int32)[None, :, None] + shift_y
    cell_x = jnp.arange(grid_cols, dtype=jnp.int32)[None, None, :] + shift_x
    inside = (cell_y >= 0) & (cell_y < grid_rows) & (cell_x >= 0) & (cell_x < grid_cols)
    patch = cell_y // PCELLS * (grid_cols // PCELLS) + cell_x // PCELLS
    cell = cell_y % PCELLS * PCELLS + cell_x % PCELLS
    return (jnp.where(inside, patch, -1).astype(jnp.int32), jnp.where(inside, cell, -1).astype(jnp.int32))


def draw_dest_patch(key, part):
    return sky_cells(key)[0]


def draw_dest_cell(key, part):
    return sky_cells(key)[1]


def touch_ends(values, key, least, high):
    place = [jax.random.randint(jax.random.fold_in(key, axis), (), 0, length) for axis, length in enumerate(values.shape)]
    longest = values.shape.index(max(values.shape))
    next_to = place[:longest] + [(place[longest] + 1) % values.shape[longest]] + place[longest + 1:]
    return values.at[tuple(place)].set(least).at[tuple(next_to)].set(high)


def shard_levels(rng, dims, cuts, smallest, top_value):
    loudness = 1.0
    for position, parts in cuts:
        draws = jax.random.uniform(jax.random.fold_in(jax.random.fold_in(rng, 6), position), (parts,), jnp.float32, smallest / len(cuts), top_value / len(cuts))
        loudness = loudness * jnp.repeat(jnp.exp(draws), dims[position] // parts).reshape((-1,) + (1,) * (len(dims) - 1 - position))
    return loudness


def gaussian(key, dims, deviation, bound, shards=(), kind=jnp.bfloat16):
    gain = shard_levels(key, dims, shards, -0.22, 0.18) if shards else 1.0
    array = jax.random.normal(key, dims, jnp.float32) * deviation * gain
    return jnp.minimum(jnp.maximum(array, -bound), bound).astype(kind)


def setup_inputs(seed: int = 0) -> dict:
    seeds = jax.random.split(jax.random.key(seed), 7)
    images = gaussian(seeds[0], (EXPOS, ROWS, COLS), 1.0, 6.0, ((0, 16), (1, 16)))
    psf_taps = jnp.clip(0.019897461 + 0.17932129 * jax.random.uniform(seeds[1], (EXPOS, 2, KTAPS), jnp.float32) ** shard_levels(seeds[1], (EXPOS, 2, KTAPS), ((0, 16),), -0.2, 0.2), 0.019897461, 0.19921875).astype(jnp.bfloat16)
    exposure_weights = jnp.clip(jnp.exp(math.log(8.0) - 2.7725887 * jax.random.uniform(seeds[2], (EXPOS,), jnp.float32) ** shard_levels(seeds[2], (EXPOS,), ((0, 16),), -0.2, 0.2)), 0.5, 8.0)
    dest_patch = draw_dest_patch(jax.random.fold_in(seeds[6], 71), 0)
    dest_cell = draw_dest_cell(jax.random.fold_in(seeds[6], 71), 0)
    shift_class = touch_ends(jax.random.randint(seeds[5], (EXPOS, 2, ROWS // TILE, COLS // TILE), 0, SHIFTS), jax.random.fold_in(seeds[5], 1), 0, SHIFTS - 1).astype(jnp.int32)
    return {"images": images, "psf_taps": psf_taps, "exposure_weights": exposure_weights, "dest_patch": dest_patch, "dest_cell": dest_cell, "shift_class": shift_class}


def lanczos_table(size, classes):
    out_pos = jnp.arange(size, dtype=jnp.float32)[None, :, None]
    src_pos = jnp.arange(size + 6, dtype=jnp.float32)[None, None, :] - 3.0
    frac = jnp.arange(classes, dtype=jnp.float32)[:, None, None] / classes
    dist = src_pos - out_pos - frac
    kernel = jnp.where(jnp.abs(dist) < 3.0, jnp.sinc(dist) * jnp.sinc(dist / 3.0), 0.0)
    kernel = kernel / jnp.sum(kernel, axis=2, keepdims=True)
    return kernel.astype(jnp.bfloat16)


def tile_windows(framed, tile, band, cols):
    padded = jnp.pad(framed, ((0, tile - 6), (3, tile - 3)))
    count_y = band // tile
    count_x = cols // tile
    width = cols + tile
    rmain = padded[:band].reshape(count_y, tile, width)
    rtail = padded[tile:tile + band].reshape(count_y, tile, width)[:, :6]
    rowwin = jnp.concatenate([rmain, rtail], axis=1)
    cmain = rowwin[:, :, :cols].reshape(count_y, tile + 6, count_x, tile)
    ctail = rowwin[:, :, tile:tile + cols].reshape(count_y, tile + 6, count_x, tile)[..., :6]
    return jnp.concatenate([cmain, ctail], axis=3)


def reference(images, psf_taps, exposure_weights, dest_patch, dest_cell, shift_class):
    table = lanczos_table(TILE, SHIFTS).astype(jnp.float32)
    reach = KTAPS // 2

    def one(carry, inputs):
        total, cover = carry
        image, taps, weight, patch, cell, classes = inputs
        taps = taps.astype(jnp.float32)
        raw = jnp.pad(image.astype(jnp.float32), ((0, 0), (reach, reach)))
        colpassed = jnp.zeros((ROWS, COLS), jnp.float32)
        for b in range(KTAPS):
            colpassed = colpassed + taps[1, b] * raw[:, b:b + COLS]
        colpassed = jnp.pad(colpassed.astype(jnp.bfloat16).astype(jnp.float32), ((reach, reach), (0, 0)))
        matched = jnp.zeros((ROWS, COLS), jnp.float32)
        for a in range(KTAPS):
            matched = matched + taps[0, a] * colpassed[a:a + ROWS]
        matched = matched.astype(jnp.bfloat16)
        framed = jnp.pad(matched, ((3, 3), (0, 0)))
        tiles = tile_windows(framed, TILE, ROWS, COLS).astype(jnp.float32)
        along_cols = table[classes[1]]
        half = jnp.einsum('yrxj,yxij->yxri', tiles, along_cols).astype(jnp.bfloat16).astype(jnp.float32)
        along_rows = table[classes[0]]
        warped = jnp.einsum('yxor,yxri->yxoi', along_rows, half).astype(jnp.bfloat16).astype(jnp.float32)
        where_to = jnp.where(patch >= 0, patch * CELLS + cell, PATCHES * CELLS).reshape(-1).astype(jnp.int32)
        total = total.at[where_to].add(weight * warped.reshape(-1, TILE, TILE), mode="drop")
        cover = cover.at[where_to].add(jnp.full(where_to.shape, weight, jnp.float32), mode="drop")
        return (total, cover), None

    start = (jnp.zeros((PATCHES * CELLS, TILE, TILE), jnp.float32), jnp.zeros((PATCHES * CELLS,), jnp.float32))
    (total, cover), unused = lax.scan(one, start, (images, psf_taps, exposure_weights, dest_patch, dest_cell, shift_class))
    coadd = total / jnp.maximum(cover, 1.0)[:, None, None]
    return coadd.reshape(PATCHES, CELLS, TILE, TILE), cover.reshape(PATCHES, CELLS)
```

```python
import jax
import jax.numpy as jnp
import numpy as np
from jax import lax
from jax.experimental import pallas as pl
from jax.experimental.pallas import tpu as pltpu
from jax.sharding import Mesh, PartitionSpec as P

TILE = 128
KTAPS = 13
SHIFTS = 8
HALO = 16
BAND = 256
COLS = 4096
STACK = BAND + 2 * HALO
BLOCKS = COLS // TILE + 1
FRAME = 144
LEAD = 119
HALF_TILES = 8
PIECE = HALF_TILES * TILE + 32
CELLROW = 4 * TILE + 16
VMEM = 50 * 1024 * 1024
f32 = jnp.float32
bf16 = jnp.bfloat16


def lanczos_tables():
    out_pos = np.arange(TILE)[None, :, None]
    src_pos = np.arange(TILE + 6)[None, None, :] - 3.0
    frac = np.arange(SHIFTS)[:, None, None] / SHIFTS
    dist = src_pos - out_pos - frac
    kernel = np.where(np.abs(dist) < 3.0, np.sinc(dist) * np.sinc(dist / 3.0), 0.0)
    kernel = kernel / np.sum(kernel, axis=2, keepdims=True)
    along_rows = np.zeros((SHIFTS + 1, TILE, FRAME), np.float32)
    along_rows[:SHIFTS, :, : TILE + 6] = kernel
    along_cols = np.zeros((SHIFTS, 2 * TILE, TILE), np.float32)
    along_cols[:, LEAD : LEAD + TILE + 6] = kernel.transpose(0, 2, 1)
    return along_rows.astype(bf16), along_cols.astype(bf16)


def banded(taps_ref, which, shape, diff):
    total = jnp.zeros(shape, f32)
    for k in range(KTAPS):
        total = jnp.where(diff == k, taps_ref[which, k], total)
    return total


def filter_kernel(pos_ref, taps_ref, top_ref, img_ref, bot_ref, out_ref, raw_ref):
    patch = pos_ref[0]
    raw_ref[:, :TILE] = jnp.zeros((STACK, TILE), bf16)
    raw_ref[:, TILE + COLS :] = jnp.zeros((STACK, TILE), bf16)
    raw_ref[:HALO, TILE : TILE + COLS] = top_ref[...]
    raw_ref[HALO : HALO + BAND, TILE : TILE + COLS] = img_ref[...]
    raw_ref[HALO + BAND :, TILE : TILE + COLS] = bot_ref[...]
    shape = (2 * TILE, TILE)
    diff = lax.broadcasted_iota(jnp.int32, shape, 0) - lax.broadcasted_iota(jnp.int32, shape, 1)
    over_cols = banded(taps_ref, 1, shape, diff).astype(bf16)
    shape = (FRAME, FRAME + 16)
    row = lax.broadcasted_iota(jnp.int32, shape, 0)
    base = banded(taps_ref, 0, shape, lax.broadcasted_iota(jnp.int32, shape, 1) - row - 7)
    over_rows = []
    for r in range(2):
        first = jnp.where(patch == 0, 3, 0) if r == 0 else 0
        last = jnp.where(patch == 15, 130, 133) if r == 1 else 133
        over_rows.append(jnp.where((row >= first) & (row <= last), base, 0.0).astype(bf16))

    def step(i, carry):
        start = pl.multiple_of(i * (3 * TILE), TILE)
        passed = [
            jnp.dot(
                raw_ref[:, pl.ds(pl.multiple_of(start + b * TILE, TILE), 2 * TILE)],
                over_cols,
                preferred_element_type=f32,
            ).astype(bf16)
            for b in range(3)
        ]
        passed = jnp.concatenate(passed, axis=1)
        for r in range(2):
            out_ref[r, :, pl.ds(start, 3 * TILE)] = jnp.dot(
                over_rows[r],
                passed[r * TILE : r * TILE + FRAME + 16],
                preferred_element_type=f32,
            ).astype(bf16)
        return carry

    lax.fori_loop(0, BLOCKS // 3, step, 0)
    lane = lax.broadcasted_iota(jnp.int32, (FRAME, TILE), 1)
    for r in range(2):
        edge = out_ref[r, :, :TILE].astype(f32)
        out_ref[r, :, :TILE] = jnp.where(lane >= 122, edge, 0.0).astype(bf16)
        edge = out_ref[r, :, COLS:].astype(f32)
        out_ref[r, :, COLS:] = jnp.where(lane < 122, edge, 0.0).astype(bf16)


def filtered(pos, taps, top, img, bot):
    smem = pl.BlockSpec(memory_space=pltpu.SMEM)
    vmem = pl.BlockSpec(memory_space=pltpu.VMEM)
    return pl.pallas_call(
        filter_kernel,
        out_shape=jax.ShapeDtypeStruct((2, FRAME, BLOCKS * TILE), bf16),
        in_specs=[smem, smem, vmem, vmem, vmem],
        out_specs=vmem,
        scratch_shapes=[pltpu.VMEM((STACK, COLS + 2 * TILE), bf16)],
        compiler_params=pltpu.CompilerParams(vmem_limit_bytes=VMEM),
        name="filter_band",
    )(pos, taps, top, img, bot)


def warp_kernel(hop, pos_ref, shift_ref, class_ref, flag_ref, weight_ref, rows_ref, cols_ref, in_ref, own_ref, sib_ref):
    core = pos_ref[1]
    dest = (pos_ref[2] + hop) % 4
    down = shift_ref[0]
    right = shift_ref[1]
    line = lax.broadcasted_iota(jnp.int32, (32, TILE), 0)
    weight = jnp.full((32, TILE), weight_ref[0], f32)
    high = weight.astype(bf16).astype(f32)
    mid = (weight - high).astype(bf16).astype(f32)
    low = weight - high - mid
    parts = jnp.where(line < 8, high, jnp.where(line < 16, mid, low))
    for side, out_ref in ((0, own_ref), (1, sib_ref)):
        half = core if side == 0 else 1 - core
        marks = jnp.zeros((32, TILE), f32)
        for r in range(2):
            for w in range(4):
                slot = r * 4 + w
                col = dest * 8 + half * 4 + w - right
                inside = (col >= 0) & (col < 32)
                col = jnp.clip(col, 0, 31)
                there = jnp.where(inside, flag_ref[r, col], 0)
                tile = in_ref[r, :, pl.ds(pl.multiple_of(col * TILE, TILE), 2 * TILE)]
                along = jnp.dot(tile, cols_ref[class_ref[1, r, col]], preferred_element_type=f32)
                picked = jnp.where(there > 0, class_ref[0, r, col], SHIFTS)
                out_ref[slot * TILE : (slot + 1) * TILE, :] = jnp.dot(
                    rows_ref[picked], along.astype(bf16), preferred_element_type=f32
                ).astype(bf16)
                marks = jnp.where((line & 7) == slot, there.astype(f32), marks)
        notes = jnp.where(line < 24, marks * parts, down.astype(f32))
        out_ref[HALF_TILES * TILE :, :] = notes.astype(bf16)


def warped(hop, pos, shift, classes, flags, weight, rows, cols, matched):
    smem = pl.BlockSpec(memory_space=pltpu.SMEM)
    vmem = pl.BlockSpec(memory_space=pltpu.VMEM)
    piece = jax.ShapeDtypeStruct((PIECE, TILE), bf16)
    return pl.pallas_call(
        lambda *refs: warp_kernel(hop, *refs),
        out_shape=(piece, piece),
        in_specs=[smem] * 5 + [vmem] * 3,
        out_specs=(vmem, vmem),
        compiler_params=pltpu.CompilerParams(vmem_limit_bytes=VMEM),
        name=f"warp_to_{hop}",
    )(pos, shift, classes, flags, weight, rows, cols, matched)


def place_kernel(pos_ref, *refs):
    pieces = refs[:8]
    main_ref, above_ref, below_ref, rows_ref = refs[8:]
    x = pos_ref[2]
    rows_ref[...] = jnp.zeros(rows_ref.shape, f32)
    for n, piece in enumerate(pieces):
        band = (x + 4 - n % 4) % 4
        notes = piece[HALF_TILES * TILE :, :].astype(f32)
        weights = notes[0:8] + notes[8:16] + notes[16:24]
        down = jnp.max(notes[24:32]).astype(jnp.int32)
        for r in range(2):
            at = 2 * band + r + down + 2
            for w in range(4):
                slot = r * 4 + w
                line = weights[slot : slot + 1]
                tile = piece[slot * TILE : (slot + 1) * TILE, :].astype(f32)
                rows_ref[at, w * TILE : (w + 1) * TILE, :] += line * tile
            rows_ref[at, 4 * TILE : 4 * TILE + 4, :] += weights[r * 4 : r * 4 + 4]
    above_ref[...] = rows_ref[0:2]
    main_ref[...] = rows_ref[2:10]
    below_ref[...] = rows_ref[10:12]


def placed_rows(pos, pieces):
    smem = pl.BlockSpec(memory_space=pltpu.SMEM)
    vmem = pl.BlockSpec(memory_space=pltpu.VMEM)

    def rows(n):
        return jax.ShapeDtypeStruct((n, CELLROW, TILE), f32)

    return pl.pallas_call(
        place_kernel,
        out_shape=(rows(8), rows(2), rows(2)),
        in_specs=[smem] + [vmem] * 8,
        out_specs=(vmem,) * 3,
        scratch_shapes=[pltpu.VMEM((12, CELLROW, TILE), f32)],
        compiler_params=pltpu.CompilerParams(vmem_limit_bytes=VMEM),
        name="place_rows",
    )(pos, *pieces)


def local(images, psf_taps, exposure_weights, dest_patch, dest_cell, shift_class):
    z, core, y, x = (lax.axis_index(a) for a in ("z", "core", "y", "x"))
    patch = y * 4 + x
    img = images[0]
    line = [(i, i + 1) for i in range(15)]
    top = lax.ppermute(img[BAND - HALO :], ("y", "x"), line)
    bot = lax.ppermute(img[:HALO], ("y", "x"), [(j, i) for i, j in line])
    pos = jnp.stack([patch, core, x]).astype(jnp.int32)
    owner = dest_patch[0]
    cell = dest_cell[0]
    flags = (owner >= 0).astype(jnp.int32)
    across = (owner & 3) * 8 + (cell & 7) - jnp.arange(32, dtype=jnp.int32)[None, :]
    along = (owner >> 2) * 8 + (cell >> 3) - jnp.arange(2, dtype=jnp.int32)[:, None] - 2 * patch
    shift = jnp.stack([jnp.max(jnp.where(flags > 0, s, -3)) for s in (along, across)])
    shift = jnp.where(shift > -3, shift, 0).astype(jnp.int32)
    rows, cols = lanczos_tables()
    matched = filtered(pos, psf_taps[0].astype(f32), top, img, bot)
    own = [None] * 4
    sib = [None] * 4
    for hop in (2, 1, 3, 0):
        stay, leave = warped(
            hop, pos, shift, shift_class[0], flags, exposure_weights, jnp.asarray(rows), jnp.asarray(cols), matched
        )
        if hop:
            own[hop] = lax.ppermute(stay, "x", [(i, (i + hop) % 4) for i in range(4)])
        else:
            own[hop] = stay
        sib[hop] = lax.ppermute(
            leave, ("core", "x"), [(c * 4 + i, (1 - c) * 4 + (i + hop) % 4) for c in range(2) for i in range(4)]
        )
    main, above, below = placed_rows(pos, own + sib)
    from_above = lax.ppermute(below, "y", [(i, i + 1) for i in range(3)])
    from_below = lax.ppermute(above, "y", [(i + 1, i) for i in range(3)])
    main = main.at[0:2].add(from_above).at[6:8].add(from_below)

    def block(i):
        return lax.dynamic_index_in_dim(main, (i + 16) % 8, 0, keepdims=False)

    up = block(z + 4)
    dn = block(z - 3)
    for s in range(4):
        up = lax.ppermute(up, "z", [(i, (i + 1) % 8) for i in range(8)])
        if s < 3:
            up = up + block(z + 3 - s)
            dn = lax.ppermute(dn, "z", [((i + 1) % 8, i) for i in range(8)])
            if s < 2:
                dn = dn + block(z - 2 + s)
    total = up + dn + block(z)
    cover = total[4 * TILE : 4 * TILE + 4, 0]
    coadd = total[: 4 * TILE].reshape(1, 4, TILE, TILE) / jnp.maximum(cover, 1.0)[None, :, None, None]
    return coadd, cover[None]


def solution(mesh):
    split = Mesh(mesh.devices.reshape(8, 2, 4, 4), ("z", "core", "y", "x"))
    visit = ("z", "core")
    patch = ("y", "x")
    placed = (
        P(visit, patch, None),
        P(visit, None, None),
        P(visit),
        P(visit, patch, None),
        P(visit, patch, None),
        P(visit, None, patch, None),
    )
    return jax.shard_map(
        local,
        mesh=split,
        in_specs=placed,
        out_specs=(P(patch, visit, None, None), P(patch, visit)),
        check_vma=False,
    )
```

```python
import math

import jax
import jax.numpy as jnp
import numpy as np
from jax import lax
from jax.experimental import pallas as pl
from jax.experimental.pallas import tpu as pltpu
from jax.sharding import Mesh, PartitionSpec as P

TILE = 128
KTAPS = 13
SHIFTS = 8
HALO = 16
BAND = 256
COLS = 4096
BLOCKS = COLS // TILE + 1
EDGE = 122
FRAME = 144
WINDOW = FRAME + 16
LEAD = 119
HALF_TILES = 8
PIECE = HALF_TILES * TILE + 32
CELLROW = 4 * TILE + 16
TOP_CODE = 32000.0
f32 = jnp.float32
bf16 = jnp.bfloat16
i16 = jnp.int16
i32 = jnp.int32
SMEM = pl.BlockSpec(memory_space=pltpu.SMEM)
VMEM = pl.BlockSpec(memory_space=pltpu.VMEM)


def call(kernel, name, out_shape, in_specs, out_specs, scratch=(), mib=8):
    return pl.pallas_call(
        kernel,
        out_shape=out_shape,
        in_specs=in_specs,
        out_specs=out_specs,
        scratch_shapes=scratch,
        compiler_params=pltpu.CompilerParams(vmem_limit_bytes=mib * 2**20),
        name=name,
    )


def lanczos_tables():
    out_pos = np.arange(TILE)[None, :, None]
    src_pos = np.arange(TILE + 6)[None, None, :] - 3.0
    frac = np.arange(SHIFTS)[:, None, None] / SHIFTS
    dist = src_pos - out_pos - frac
    kernel = np.where(np.abs(dist) < 3.0, np.sinc(dist) * np.sinc(dist / 3.0), 0.0)
    kernel = kernel / np.sum(kernel, axis=2, keepdims=True)
    along_rows = np.zeros((SHIFTS + 1, TILE, FRAME), np.float32)
    along_rows[:SHIFTS, :, : TILE + 6] = kernel
    along_cols = np.zeros((SHIFTS, 2 * TILE, TILE), np.float32)
    along_cols[:, LEAD : LEAD + TILE + 6] = kernel.transpose(0, 2, 1)
    return along_rows.astype(bf16), along_cols.astype(bf16)


def banded(taps, shape, base):
    diff = lax.broadcasted_iota(i32, shape, 0) - lax.broadcasted_iota(i32, shape, 1) + base
    total = jnp.zeros(shape, f32)
    for k in range(KTAPS):
        total = jnp.where(diff == k, taps[:, k : k + 1], total)
    return total


def columns_kernel(taps_ref, patch_ref, cell_ref, img_ref, out_ref, info_ref):
    over_cols = banded(taps_ref[0].astype(f32)[1:2], (2 * TILE, TILE), 0)
    lane = lax.broadcasted_iota(i32, (TILE, TILE), 1)
    first = jnp.where(lane >= EDGE, over_cols[TILE:], 0.0).astype(bf16)
    last = jnp.where(lane < EDGE, over_cols[:TILE], 0.0).astype(bf16)
    over_cols = over_cols.astype(bf16)
    for b in range(BLOCKS):
        if b == 0:
            window, weights = img_ref[0, :, :TILE], first
        elif b == BLOCKS - 1:
            window, weights = img_ref[0, :, COLS - TILE :], last
        else:
            window, weights = img_ref[0, :, (b - 1) * TILE : (b + 1) * TILE], over_cols
        out_ref[:, b * TILE : (b + 1) * TILE] = jnp.dot(window, weights, preferred_element_type=f32).astype(bf16)
    owner = patch_ref[0]
    cell = cell_ref[0]
    row0 = 2 * (lax.axis_index("y") * 4 + lax.axis_index("x"))
    down = (owner >> 2) * 8 + (cell >> 3) - lax.broadcasted_iota(i32, owner.shape, 0) - row0
    right = (owner & 3) * 8 + (cell & 7) - lax.broadcasted_iota(i32, owner.shape, 1)
    for n, offset in enumerate((down, right)):
        most = jnp.max(jnp.where(owner >= 0, offset.astype(f32), -8.0)).astype(i32)
        info_ref[n] = jnp.where(most > -8, most, 0)


def rows_kernel(taps_ref, top_ref, bot_ref, passed_ref, out_ref, window_ref, edge_ref):
    patch = lax.axis_index("y") * 4 + lax.axis_index("x")
    taps = taps_ref[0].astype(f32)
    over_cols = banded(taps[1:2], (2 * TILE, TILE), 0).astype(bf16)
    halo = 2 * HALO
    for b in range(BLOCKS):
        for side in range(2):
            k = b - 1 + side
            at = (slice(b * halo, b * halo + HALO), slice(side * TILE, (side + 1) * TILE))
            at_bot = (slice(b * halo + HALO, (b + 1) * halo), at[1])
            if 0 <= k < BLOCKS - 1:
                window_ref[at] = top_ref[:, k * TILE : (k + 1) * TILE]
                window_ref[at_bot] = bot_ref[:, k * TILE : (k + 1) * TILE]
            else:
                window_ref[at] = jnp.zeros((HALO, TILE), bf16)
                window_ref[at_bot] = jnp.zeros((HALO, TILE), bf16)
    lane = lax.broadcasted_iota(i32, (halo, TILE), 1)
    for part in range(3):
        each = BLOCKS // 3
        got = jnp.dot(
            window_ref[part * each * halo : (part + 1) * each * halo], over_cols, preferred_element_type=f32
        )
        for n in range(each):
            b = part * each + n
            rows = got[n * halo : (n + 1) * halo]
            if b == 0:
                rows = jnp.where(lane >= EDGE, rows, 0.0)
            if b == BLOCKS - 1:
                rows = jnp.where(lane < EDGE, rows, 0.0)
            edge_ref[:, b * TILE : (b + 1) * TILE] = rows.astype(bf16)
    shape = (FRAME, WINDOW)
    row = lax.broadcasted_iota(i32, shape, 0)
    base = jnp.zeros(shape, f32)
    step = lax.broadcasted_iota(i32, shape, 1) - row - 7
    for k in range(KTAPS):
        base = jnp.where(step == k, taps[0:1, k : k + 1], base)
    low = jnp.where(patch == 0, 3, 0)
    high = jnp.where(patch == 15, 130, 133)
    over_rows = (
        jnp.where((row >= low) & (row <= 133), base, 0.0).astype(bf16),
        jnp.where(row <= high, base, 0.0).astype(bf16),
    )
    for n in range(BLOCKS // 3):
        at = slice(n * 3 * TILE, (n + 1) * 3 * TILE)
        upper = jnp.concatenate([edge_ref[:HALO, at], passed_ref[:FRAME, at]], axis=0)
        lower = jnp.concatenate([passed_ref[BAND - FRAME :, at], edge_ref[HALO:, at]], axis=0)
        for r, window in enumerate((upper, lower)):
            out_ref[r, :, at] = jnp.dot(over_rows[r], window, preferred_element_type=f32).astype(bf16)


def warp_kernel(hop, info_ref, patch_ref, class_ref, weight_ref, rows_ref, cols_ref, in_ref, own_ref, sib_ref, half_ref):
    core = lax.axis_index("core")
    dest = (lax.axis_index("x") + hop) & 3
    line = lax.broadcasted_iota(i32, (32, TILE), 0)
    weight = jnp.full((32, TILE), weight_ref[0], f32)
    high = weight.astype(bf16).astype(f32)
    mid = (weight - high).astype(bf16).astype(f32)
    low = weight - high - mid
    parts = jnp.where(line < 8, high, jnp.where(line < 16, mid, low))
    down = info_ref[0].astype(f32)
    plan = []
    for side, out_ref in enumerate((own_ref, sib_ref)):
        half = core if side == 0 else 1 - core
        marks = jnp.zeros((32, TILE), f32)
        for slot in range(HALF_TILES):
            r, w = divmod(slot, 4)
            col = dest * 8 + half * 4 + w - info_ref[1]
            inside = (col >= 0) & (col < 32)
            col = jnp.clip(col, 0, 31)
            there = inside & (patch_ref[0, r, col] >= 0)
            plan.append((out_ref, slot, r, col, jnp.where(there, class_ref[0, 0, r, col], SHIFTS)))
            marks = jnp.where((line & 7) == slot, jnp.where(there, 1.0, 0.0), marks)
        out_ref[HALF_TILES * TILE :, :] = jnp.where(line < 24, marks * parts, down).astype(bf16)
    for n, (out_ref, slot, r, col, picked) in enumerate(plan):
        tile = in_ref[r, :, pl.ds(pl.multiple_of(col * TILE, TILE), 2 * TILE)]
        half_ref[n] = jnp.dot(tile, cols_ref[class_ref[0, 1, r, col]], preferred_element_type=f32).astype(bf16)
    for n, (out_ref, slot, r, col, picked) in enumerate(plan):
        out_ref[slot * TILE : (slot + 1) * TILE, :] = jnp.dot(
            rows_ref[picked], half_ref[n], preferred_element_type=f32
        ).astype(bf16)


def encode(cells, weights, out_ref, start):
    line = lax.broadcasted_iota(i32, (16, TILE), 0)
    notes = jnp.zeros((16, TILE), f32)
    for w in range(4):
        cell = cells[w]
        most = jnp.max(jnp.max(jnp.abs(cell), axis=0, keepdims=True), axis=1, keepdims=True)
        level = jnp.ceil(jnp.log(jnp.maximum(most, 1e-33)) * (128.0 / math.log(2.0)))
        code = jnp.floor(cell * (TOP_CODE * jnp.exp(level * (-math.log(2.0) / 128.0))) + 0.5)
        out_ref[start + w * TILE : start + (w + 1) * TILE, :] = code.astype(i32).astype(i16)
        whole = jnp.floor(weights[w : w + 1] * 128.0)
        rest = jnp.floor((weights[w : w + 1] * 128.0 - whole) * 32767.0 + 0.5)
        notes = jnp.where(line == w, level, notes)
        notes = jnp.where(line == 4 + w, whole, notes)
        notes = jnp.where(line == 8 + w, rest, notes)
    out_ref[start + 4 * TILE : start + CELLROW, :] = notes.astype(i32).astype(i16)


def decode(in_ref, start):
    notes = in_ref[start + 4 * TILE : start + CELLROW, :].astype(i32).astype(f32)
    cells = []
    for w in range(4):
        scale = jnp.exp(notes[w : w + 1] * (math.log(2.0) / 128.0)) * (1.0 / TOP_CODE)
        code = in_ref[start + w * TILE : start + (w + 1) * TILE, :].astype(i32).astype(f32)
        cells.append(code * scale)
    return cells, (notes[4:8] + notes[8:12] * (1.0 / 32767.0)) * (1.0 / 128.0)


def held(ref, at):
    cells = [ref[at, w * TILE : (w + 1) * TILE, :] for w in range(4)]
    return cells, ref[at, 4 * TILE : 4 * TILE + 4, :]


def added(*parts):
    cells = [sum(p[0][w] for p in parts[1:]) + parts[0][0][w] for w in range(4)]
    return cells, sum(p[1] for p in parts[1:]) + parts[0][1]


def place_kernel(*refs):
    pieces = refs[:8]
    main_ref, above_ref, below_ref, rows_ref = refs[8:]
    x = lax.axis_index("x")
    rows_ref[...] = jnp.zeros(rows_ref.shape, f32)
    for n, piece in enumerate(pieces):
        band = (x + 4 - n % 4) & 3
        notes = piece[HALF_TILES * TILE :, :].astype(f32)
        weights = notes[0:8] + notes[8:16] + notes[16:24]
        down = jnp.max(notes[24:32]).astype(i32)
        for r in range(2):
            at = 2 * band + r + down + 2
            for w in range(4):
                slot = r * 4 + w
                tile = piece[slot * TILE : (slot + 1) * TILE, :].astype(f32)
                rows_ref[at, w * TILE : (w + 1) * TILE, :] += weights[slot : slot + 1] * tile
            rows_ref[at, 4 * TILE : 4 * TILE + 4, :] += weights[r * 4 : r * 4 + 4]
    for r in range(2):
        encode(*held(rows_ref, r), above_ref, r * CELLROW)
        encode(*held(rows_ref, 10 + r), below_ref, r * CELLROW)
    main_ref[...] = rows_ref[2:10]


def merge_kernel(in_ref, above_ref, below_ref, main_ref, up_ref, dn_ref, far_ref):
    main_ref[...] = in_ref[...]
    for r in range(2):
        for ref, at in ((above_ref, r), (below_ref, 6 + r)):
            cells, weights = added(held(in_ref, at), decode(ref, r * CELLROW))
            for w in range(4):
                main_ref[at, w * TILE : (w + 1) * TILE, :] = cells[w]
            main_ref[at, 4 * TILE : 4 * TILE + 4, :] = weights
    z = lax.axis_index("z")
    encode(*held(main_ref, (z + 3) & 7), up_ref, 0)
    encode(*held(main_ref, (z + 5) & 7), dn_ref, 0)
    encode(*held(main_ref, (z + 4) & 7), far_ref, 0)


def step_kernel(ahead, main_ref, in_ref, out_ref):
    at = (lax.axis_index("z") + 8 + ahead) & 7
    encode(*added(held(main_ref, at), decode(in_ref, 0)), out_ref, 0)


def finish_kernel(main_ref, up_ref, dn_ref, far_ref, coadd_ref, cover_ref):
    z = lax.axis_index("z")
    cells, weights = added(held(main_ref, z), decode(up_ref, 0), decode(dn_ref, 0), decode(far_ref, 0))
    lane = lax.broadcasted_iota(i32, (1, TILE), 1)
    cover = jnp.zeros((1, TILE), f32)
    for w in range(4):
        coadd_ref[0, w] = cells[w] / jnp.maximum(weights[w : w + 1], 1.0)
        cover = jnp.where(lane == w, weights[w : w + 1], cover)
    cover_ref[...] = cover[:, :4]


def local(images, psf_taps, exposure_weights, dest_patch, dest_cell, shift_class):
    shape = jax.ShapeDtypeStruct
    line = [(i, i + 1) for i in range(15)]
    top = lax.ppermute(images[0, BAND - HALO :], ("y", "x"), line)
    bot = lax.ppermute(images[0, :HALO], ("y", "x"), [(j, i) for i, j in line])
    rows, cols = (jnp.asarray(t) for t in lanczos_tables())
    passed, info = call(
        columns_kernel,
        "columns",
        (shape((BAND, BLOCKS * TILE), bf16), shape((2,), i32)),
        [VMEM] * 4,
        (VMEM, SMEM),
    )(psf_taps, dest_patch, dest_cell, images)
    matched = call(
        rows_kernel,
        "rows",
        shape((2, FRAME, BLOCKS * TILE), bf16),
        [VMEM] * 4,
        VMEM,
        [pltpu.VMEM((BLOCKS * 2 * HALO, 2 * TILE), bf16), pltpu.VMEM((2 * HALO, BLOCKS * TILE), bf16)],
    )(psf_taps, top, bot, passed)
    piece = shape((PIECE, TILE), bf16)
    own = [None] * 4
    sib = [None] * 4
    for hop in (2, 1, 3, 0):
        stay, leave = call(
            lambda *refs, hop=hop: warp_kernel(hop, *refs),
            f"warp_{hop}",
            (piece, piece),
            [SMEM] * 4 + [VMEM] * 3,
            (VMEM, VMEM),
            [pltpu.VMEM((2 * HALF_TILES, FRAME, TILE), bf16)],
        )(info, dest_patch, shift_class, exposure_weights, rows, cols, matched)
        if hop:
            own[hop] = lax.ppermute(stay, "x", [(i, (i + hop) % 4) for i in range(4)])
        else:
            own[hop] = stay
        sib[hop] = lax.ppermute(
            leave, ("core", "x"), [(c * 4 + i, (1 - c) * 4 + (i + hop) % 4) for c in range(2) for i in range(4)]
        )
    held_rows = shape((8, CELLROW, TILE), f32)
    spill = shape((2 * CELLROW, TILE), i16)
    coded = shape((CELLROW, TILE), i16)
    main, above, below = call(
        place_kernel, "place", (held_rows, spill, spill), [VMEM] * 8, (VMEM,) * 3, [pltpu.VMEM((12, CELLROW, TILE), f32)]
    )(*own, *sib)
    from_above = lax.ppermute(below, "y", [(i, i + 1) for i in range(3)])
    from_below = lax.ppermute(above, "y", [(i + 1, i) for i in range(3)])
    main, up, dn, far = call(
        merge_kernel, "merge", (held_rows, coded, coded, coded), [VMEM] * 3, (VMEM,) * 4
    )(main, from_above, from_below)
    far = lax.ppermute(far, "z", [(i, (i + 4) % 8) for i in range(8)])
    for s in (2, 1, 0):
        up = lax.ppermute(up, "z", [(i, (i + 1) % 8) for i in range(8)])
        dn = lax.ppermute(dn, "z", [((i + 1) % 8, i) for i in range(8)])
        if s:
            up = call(lambda *refs, s=s: step_kernel(s, *refs), f"up_{s}", coded, [VMEM] * 2, VMEM)(main, up)
            dn = call(lambda *refs, s=s: step_kernel(-s, *refs), f"down_{s}", coded, [VMEM] * 2, VMEM)(main, dn)
    return call(
        finish_kernel, "finish", (shape((1, 4, TILE, TILE), f32), shape((1, 4), f32)), [VMEM] * 4, (VMEM, VMEM)
    )(main, up, dn, far)


def solution(mesh):
    split = Mesh(mesh.devices.reshape(8, 2, 4, 4), ("z", "core", "y", "x"))
    visit = ("z", "core")
    patch = ("y", "x")
    placed = (
        P(visit, patch, None),
        P(visit, None, None),
        P(visit),
        P(visit, patch, None),
        P(visit, patch, None),
        P(visit, None, patch, None),
    )
    return jax.shard_map(
        local,
        mesh=split,
        in_specs=placed,
        out_specs=(P(patch, visit, None, None), P(patch, visit)),
        check_vma=False,
    )
```

```python
import math

import jax
import jax.numpy as jnp
import numpy as np
from jax import lax
from jax.experimental import pallas as pl
from jax.experimental.pallas import tpu as pltpu
from jax.sharding import Mesh, PartitionSpec as P

TILE = 128
KTAPS = 13
SHIFTS = 8
HALO = 16
BAND = 256
COLS = 4096
BLOCKS = COLS // TILE + 1
EDGE = 122
FRAME = 144
WINDOW = FRAME + 16
LEAD = 119
HALF_TILES = 8
PIECE = HALF_TILES * TILE + 32
CELLROW = 4 * TILE + 16
TOP_CODE = 32000.0
HOPS = ((1, 3), (2, 0))
WARP_COST = 0
CHAIN = 3
FIRST = (CHAIN, -CHAIN, 4) + tuple(sign * d for d in range(CHAIN + 1, 4) for sign in (1, -1))
f32 = jnp.float32
bf16 = jnp.bfloat16
i16 = jnp.int16
i32 = jnp.int32
SMEM = pl.BlockSpec(memory_space=pltpu.SMEM)
VMEM = pl.BlockSpec(memory_space=pltpu.VMEM)
HBM = pl.BlockSpec(memory_space=pltpu.HBM)


def call(kernel, name, out_shape, in_specs, out_specs, scratch=(), mib=8, flops=0):
    return pl.pallas_call(
        kernel,
        out_shape=out_shape,
        in_specs=in_specs,
        out_specs=out_specs,
        scratch_shapes=scratch,
        compiler_params=pltpu.CompilerParams(vmem_limit_bytes=mib * 2**20),
        cost_estimate=pl.CostEstimate(flops=flops, transcendentals=0, bytes_accessed=0) if flops else None,
        name=name,
    )


def lanczos_tables():
    out_pos = np.arange(TILE)[None, :, None]
    src_pos = np.arange(TILE + 6)[None, None, :] - 3.0
    frac = np.arange(SHIFTS)[:, None, None] / SHIFTS
    dist = src_pos - out_pos - frac
    kernel = np.where(np.abs(dist) < 3.0, np.sinc(dist) * np.sinc(dist / 3.0), 0.0)
    kernel = kernel / np.sum(kernel, axis=2, keepdims=True)
    along_rows = np.zeros((SHIFTS + 1, TILE, FRAME), np.float32)
    along_rows[:SHIFTS, :, : TILE + 6] = kernel
    along_cols = np.zeros((SHIFTS, 2 * TILE, TILE), np.float32)
    along_cols[:, LEAD : LEAD + TILE + 6] = kernel.transpose(0, 2, 1)
    return along_rows.astype(bf16), along_cols.astype(bf16)


def banded(taps, shape, base):
    diff = lax.broadcasted_iota(i32, shape, 0) - lax.broadcasted_iota(i32, shape, 1) + base
    total = jnp.zeros(shape, f32)
    for k in range(KTAPS):
        total = jnp.where(diff == k, taps[:, k : k + 1], total)
    return total


def columns_kernel(taps_hbm, patch_hbm, cell_hbm, img_hbm, out_ref, info_ref, taps_ref, patch_ref, cell_ref, img_ref, sems):
    small = [
        pltpu.make_async_copy(src.at[0], dst, sems.at[n])
        for n, (src, dst) in enumerate(((taps_hbm, taps_ref), (patch_hbm, patch_ref), (cell_hbm, cell_ref)))
    ]
    quarter = COLS // 4
    parts = []
    for n in range(4):
        at = slice(n * quarter, (n + 1) * quarter)
        parts.append(pltpu.make_async_copy(img_hbm.at[0, :, at], img_ref.at[:, at], sems.at[3 + n]))
    for copy in small + parts:
        copy.start()
    for copy in small:
        copy.wait()
    over_cols = banded(taps_ref[...].astype(f32)[1:2], (2 * TILE, TILE), 0)
    lane = lax.broadcasted_iota(i32, (TILE, TILE), 1)
    first = jnp.where(lane >= EDGE, over_cols[TILE:], 0.0).astype(bf16)
    last = jnp.where(lane < EDGE, over_cols[:TILE], 0.0).astype(bf16)
    over_cols = over_cols.astype(bf16)
    owner = patch_ref[...]
    cell = cell_ref[...]
    row0 = 2 * (lax.axis_index("y") * 4 + lax.axis_index("x"))
    down = (owner >> 2) * 8 + (cell >> 3) - lax.broadcasted_iota(i32, owner.shape, 0) - row0
    right = (owner & 3) * 8 + (cell & 7) - lax.broadcasted_iota(i32, owner.shape, 1)
    for n, offset in enumerate((down, right)):
        most = jnp.max(jnp.where(owner >= 0, offset.astype(f32), -8.0)).astype(i32)
        info_ref[n] = jnp.where(most > -8, jnp.clip(most, -2, 2), 0)
    for b in range(BLOCKS):
        if b % 8 == 0 and b < BLOCKS - 1:
            parts[b // 8].wait()
        if b == 0:
            window, weights = img_ref[:, :TILE], first
        elif b == BLOCKS - 1:
            window, weights = img_ref[:, COLS - TILE :], last
        else:
            window, weights = img_ref[:, (b - 1) * TILE : (b + 1) * TILE], over_cols
        out_ref[:, b * TILE : (b + 1) * TILE] = jnp.dot(window, weights, preferred_element_type=f32).astype(bf16)


def rows_kernel(taps_ref, top_ref, bot_ref, passed_ref, out_ref, window_ref, edge_ref):
    patch = lax.axis_index("y") * 4 + lax.axis_index("x")
    taps = taps_ref[0].astype(f32)
    over_cols = banded(taps[1:2], (2 * TILE, TILE), 0).astype(bf16)
    halo = 2 * HALO
    for b in range(BLOCKS):
        for side in range(2):
            k = b - 1 + side
            at = (slice(b * halo, b * halo + HALO), slice(side * TILE, (side + 1) * TILE))
            at_bot = (slice(b * halo + HALO, (b + 1) * halo), at[1])
            if 0 <= k < BLOCKS - 1:
                window_ref[at] = top_ref[:, k * TILE : (k + 1) * TILE]
                window_ref[at_bot] = bot_ref[:, k * TILE : (k + 1) * TILE]
            else:
                window_ref[at] = jnp.zeros((HALO, TILE), bf16)
                window_ref[at_bot] = jnp.zeros((HALO, TILE), bf16)
    lane = lax.broadcasted_iota(i32, (halo, TILE), 1)
    for part in range(3):
        each = BLOCKS // 3
        got = jnp.dot(
            window_ref[part * each * halo : (part + 1) * each * halo], over_cols, preferred_element_type=f32
        )
        for n in range(each):
            b = part * each + n
            rows = got[n * halo : (n + 1) * halo]
            if b == 0:
                rows = jnp.where(lane >= EDGE, rows, 0.0)
            if b == BLOCKS - 1:
                rows = jnp.where(lane < EDGE, rows, 0.0)
            edge_ref[:, b * TILE : (b + 1) * TILE] = rows.astype(bf16)
    shape = (FRAME, WINDOW)
    row = lax.broadcasted_iota(i32, shape, 0)
    base = jnp.zeros(shape, f32)
    step = lax.broadcasted_iota(i32, shape, 1) - row - 7
    for k in range(KTAPS):
        base = jnp.where(step == k, taps[0:1, k : k + 1], base)
    low = jnp.where(patch == 0, 3, 0)
    high = jnp.where(patch == 15, 130, 133)
    over_rows = (
        jnp.where((row >= low) & (row <= 133), base, 0.0).astype(bf16),
        jnp.where(row <= high, base, 0.0).astype(bf16),
    )
    for n in range(BLOCKS // 3):
        at = slice(n * 3 * TILE, (n + 1) * 3 * TILE)
        upper = jnp.concatenate([edge_ref[:HALO, at], passed_ref[:FRAME, at]], axis=0)
        lower = jnp.concatenate([passed_ref[BAND - FRAME :, at], edge_ref[HALO:, at]], axis=0)
        for r, window in enumerate((upper, lower)):
            out_ref[r, :, at] = jnp.dot(over_rows[r], window, preferred_element_type=f32).astype(bf16)


def warp_kernel(hops, info_ref, patch_ref, class_ref, weight_ref, rows_ref, cols_ref, in_ref, *refs):
    out_refs, half_ref = refs[:-1], refs[-1]
    core = lax.axis_index("core")
    line = lax.broadcasted_iota(i32, (32, TILE), 0)
    weight = jnp.full((32, TILE), weight_ref[0], f32)
    high = weight.astype(bf16).astype(f32)
    mid = (weight - high).astype(bf16).astype(f32)
    low = weight - high - mid
    parts = jnp.where(line < 8, high, jnp.where(line < 16, mid, low))
    down = info_ref[0].astype(f32)
    plan = []
    for n, out_ref in enumerate(out_refs):
        dest = (lax.axis_index("x") + hops[n // 2]) & 3
        half = core if n % 2 == 0 else 1 - core
        marks = jnp.zeros((32, TILE), f32)
        for slot in range(HALF_TILES):
            r, w = divmod(slot, 4)
            col = dest * 8 + half * 4 + w - info_ref[1]
            inside = (col >= 0) & (col < 32)
            col = jnp.clip(col, 0, 31)
            there = inside & (patch_ref[0, r, col] >= 0)
            plan.append((out_ref, slot, r, col, jnp.where(there, class_ref[0, 0, r, col], SHIFTS)))
            marks = jnp.where((line & 7) == slot, jnp.where(there, 1.0, 0.0), marks)
        out_ref[HALF_TILES * TILE :, :] = jnp.where(line < 24, marks * parts, down).astype(bf16)
    for n, (out_ref, slot, r, col, picked) in enumerate(plan):
        tile = in_ref[r, :, pl.ds(pl.multiple_of(col * TILE, TILE), 2 * TILE)]
        half_ref[n] = jnp.dot(tile, cols_ref[class_ref[0, 1, r, col]], preferred_element_type=f32).astype(bf16)
    for n, (out_ref, slot, r, col, picked) in enumerate(plan):
        out_ref[slot * TILE : (slot + 1) * TILE, :] = jnp.dot(
            rows_ref[picked], half_ref[n], preferred_element_type=f32
        ).astype(bf16)


def encode(cells, weights, out_ref, start):
    line = lax.broadcasted_iota(i32, (16, TILE), 0)
    notes = jnp.zeros((16, TILE), f32)
    for w in range(4):
        cell = cells[w]
        most = jnp.max(jnp.max(jnp.abs(cell), axis=0, keepdims=True), axis=1, keepdims=True)
        level = jnp.ceil(jnp.log(jnp.maximum(most, 1e-33)) * (128.0 / math.log(2.0)))
        code = jnp.floor(cell * (TOP_CODE * jnp.exp(level * (-math.log(2.0) / 128.0))) + 0.5)
        out_ref[start + w * TILE : start + (w + 1) * TILE, :] = code.astype(i32).astype(i16)
        whole = jnp.floor(weights[w : w + 1] * 128.0)
        rest = jnp.floor((weights[w : w + 1] * 128.0 - whole) * 32767.0 + 0.5)
        notes = jnp.where(line == w, level, notes)
        notes = jnp.where(line == 4 + w, whole, notes)
        notes = jnp.where(line == 8 + w, rest, notes)
    out_ref[start + 4 * TILE : start + CELLROW, :] = notes.astype(i32).astype(i16)


def decode(in_ref, start):
    notes = in_ref[start + 4 * TILE : start + CELLROW, :].astype(i32).astype(f32)
    cells = []
    for w in range(4):
        scale = jnp.exp(notes[w : w + 1] * (math.log(2.0) / 128.0)) * (1.0 / TOP_CODE)
        code = in_ref[start + w * TILE : start + (w + 1) * TILE, :].astype(i32).astype(f32)
        cells.append(code * scale)
    return cells, (notes[4:8] + notes[8:12] * (1.0 / 32767.0)) * (1.0 / 128.0)


def held(ref, at):
    cells = [ref[at, w * TILE : (w + 1) * TILE, :] for w in range(4)]
    return cells, ref[at, 4 * TILE : 4 * TILE + 4, :]


def added(*parts):
    cells = [sum(p[0][w] for p in parts[1:]) + parts[0][0][w] for w in range(4)]
    return cells, sum(p[1] for p in parts[1:]) + parts[0][1]


def place_kernel(*refs):
    pieces = refs[:8]
    main_ref, above_ref, below_ref, rows_ref = refs[8:]
    x = lax.axis_index("x")
    rows_ref[...] = jnp.zeros(rows_ref.shape, f32)
    for n, piece in enumerate(pieces):
        band = (x + 4 - n % 4) & 3
        notes = piece[HALF_TILES * TILE :, :].astype(f32)
        weights = notes[0:8] + notes[8:16] + notes[16:24]
        down = jnp.max(notes[24:32]).astype(i32)
        for r in range(2):
            at = 2 * band + r + down + 2
            for w in range(4):
                slot = r * 4 + w
                tile = piece[slot * TILE : (slot + 1) * TILE, :].astype(f32)
                rows_ref[at, w * TILE : (w + 1) * TILE, :] += weights[slot : slot + 1] * tile
            rows_ref[at, 4 * TILE : 4 * TILE + 4, :] += weights[r * 4 : r * 4 + 4]
    for r in range(2):
        encode(*held(rows_ref, r), above_ref, r * CELLROW)
        encode(*held(rows_ref, 10 + r), below_ref, r * CELLROW)
    main_ref[...] = rows_ref[2:10]


def merge_kernel(in_ref, above_ref, below_ref, main_ref, *outs):
    main_ref[...] = in_ref[...]
    for r in range(2):
        for ref, at in ((above_ref, r), (below_ref, 6 + r)):
            cells, weights = added(held(in_ref, at), decode(ref, r * CELLROW))
            for w in range(4):
                main_ref[at, w * TILE : (w + 1) * TILE, :] = cells[w]
            main_ref[at, 4 * TILE : 4 * TILE + 4, :] = weights
    z = lax.axis_index("z")
    for ahead, out_ref in zip(FIRST, outs):
        encode(*held(main_ref, (z + 8 + ahead) & 7), out_ref, 0)


def step_kernel(ahead, main_ref, in_ref, out_ref):
    at = (lax.axis_index("z") + 8 + ahead) & 7
    encode(*added(held(main_ref, at), decode(in_ref, 0)), out_ref, 0)


def finish_kernel(main_ref, *refs):
    ins, (coadd_ref, cover_ref) = refs[:-2], refs[-2:]
    z = lax.axis_index("z")
    cells, weights = added(held(main_ref, z), *[decode(ref, 0) for ref in ins])
    lane = lax.broadcasted_iota(i32, (1, TILE), 1)
    cover = jnp.zeros((1, TILE), f32)
    for w in range(4):
        coadd_ref[0, w] = cells[w] / jnp.maximum(weights[w : w + 1], 1.0)
        cover = jnp.where(lane == w, weights[w : w + 1], cover)
    cover_ref[...] = cover[:, :4]


def local(images, psf_taps, exposure_weights, dest_patch, dest_cell, shift_class):
    shape = jax.ShapeDtypeStruct
    line = [(i, i + 1) for i in range(15)]
    top = lax.ppermute(images[0, BAND - HALO :], ("y", "x"), line)
    bot = lax.ppermute(images[0, :HALO], ("y", "x"), [(j, i) for i, j in line])
    rows, cols = (jnp.asarray(t) for t in lanczos_tables())
    passed, info = call(
        columns_kernel,
        "columns",
        (shape((BAND, BLOCKS * TILE), bf16), shape((2,), i32)),
        [HBM] * 4,
        (VMEM, SMEM),
        [
            pltpu.VMEM((2, KTAPS), bf16),
            pltpu.VMEM((2, COLS // TILE), i32),
            pltpu.VMEM((2, COLS // TILE), i32),
            pltpu.VMEM((BAND, COLS), bf16),
            pltpu.SemaphoreType.DMA((7,)),
        ],
    )(*(pltpu.with_memory_space_constraint(a, pltpu.HBM) for a in (psf_taps, dest_patch, dest_cell, images)))
    matched = call(
        rows_kernel,
        "rows",
        shape((2, FRAME, BLOCKS * TILE), bf16),
        [VMEM] * 4,
        VMEM,
        [pltpu.VMEM((BLOCKS * 2 * HALO, 2 * TILE), bf16), pltpu.VMEM((2 * HALO, BLOCKS * TILE), bf16)],
    )(psf_taps, top, bot, passed)
    piece = shape((PIECE, TILE), bf16)
    own = [None] * 4
    sib = [None] * 4
    for hops in HOPS:
        outs = call(
            lambda *refs, hops=hops: warp_kernel(hops, *refs),
            "warp_" + "".join(str(h) for h in hops),
            (piece,) * (2 * len(hops)),
            [SMEM] * 4 + [VMEM] * 3,
            (VMEM,) * (2 * len(hops)),
            [pltpu.VMEM((2 * HALF_TILES * len(hops), FRAME, TILE), bf16)],
            flops=WARP_COST,
        )(info, dest_patch, shift_class, exposure_weights, rows, cols, matched)
        for n, hop in enumerate(hops):
            own[hop] = outs[2 * n]
            if hop:
                own[hop] = lax.ppermute(own[hop], "x", [(i, (i + hop) % 4) for i in range(4)])
            sib[hop] = lax.ppermute(
                outs[2 * n + 1],
                ("core", "x"),
                [(c * 4 + i, (1 - c) * 4 + (i + hop) % 4) for c in range(2) for i in range(4)],
            )
    held_rows = shape((8, CELLROW, TILE), f32)
    spill = shape((2 * CELLROW, TILE), i16)
    coded = shape((CELLROW, TILE), i16)
    main, above, below = call(
        place_kernel, "place", (held_rows, spill, spill), [VMEM] * 8, (VMEM,) * 3, [pltpu.VMEM((12, CELLROW, TILE), f32)]
    )(*own, *sib)
    from_above = lax.ppermute(below, "y", [(i, i + 1) for i in range(3)])
    from_below = lax.ppermute(above, "y", [(i + 1, i) for i in range(3)])
    main, *first = call(merge_kernel, "merge", (held_rows,) + (coded,) * len(FIRST), [VMEM] * 3, (VMEM,) * (1 + len(FIRST)))(
        main, from_above, from_below
    )

    def along_z(block, hops):
        return lax.ppermute(block, "z", [(i, (i + hops) % 8) for i in range(8)])

    up, dn = first[:2]
    for s in range(CHAIN - 1, -1, -1):
        up, dn = along_z(up, 1), along_z(dn, -1)
        if s:
            up = call(lambda *refs, s=s: step_kernel(s, *refs), f"up_{s}", coded, [VMEM] * 2, VMEM)(main, up)
            dn = call(lambda *refs, s=s: step_kernel(-s, *refs), f"down_{s}", coded, [VMEM] * 2, VMEM)(main, dn)
    far = [along_z(block, ahead) for ahead, block in zip(FIRST[2:], first[2:])]
    return call(
        finish_kernel,
        "finish",
        (shape((1, 4, TILE, TILE), f32), shape((1, 4), f32)),
        [VMEM] * (3 + len(far)),
        (VMEM, VMEM),
    )(main, up, dn, *far)


def solution(mesh):
    split = Mesh(mesh.devices.reshape(8, 2, 4, 4), ("z", "core", "y", "x"))
    visit = ("z", "core")
    patch = ("y", "x")
    placed = (
        P(visit, patch, None),
        P(visit, None, None),
        P(visit),
        P(visit, patch, None),
        P(visit, patch, None),
        P(visit, None, patch, None),
    )
    return jax.shard_map(
        local,
        mesh=split,
        in_specs=placed,
        out_specs=(P(patch, visit, None, None), P(patch, visit)),
        check_vma=False,
    )
```

```python
import math

import jax
import jax.numpy as jnp
import numpy as np
from jax import lax
from jax.experimental import pallas as pl
from jax.experimental.pallas import tpu as pltpu
from jax.sharding import Mesh, PartitionSpec as P

TILE = 128
KTAPS = 13
SHIFTS = 8
HALO = 16
BAND = 256
COLS = 4096
BLOCKS = COLS // TILE + 1
EDGE = 122
FRAME = 144
WINDOW = FRAME + 16
LEAD = 119
HALF_TILES = 8
PIECE = HALF_TILES * TILE + 32
CELLROW = 4 * TILE + 16
TOP_CODE = 32000.0
HOPS = ((1, 3), (2, 0))
CHAIN = 3
FIRST = (CHAIN, -CHAIN, 4) + tuple(sign * d for d in range(CHAIN + 1, 4) for sign in (1, -1))
f32 = jnp.float32
bf16 = jnp.bfloat16
i16 = jnp.int16
i32 = jnp.int32
SMEM = pl.BlockSpec(memory_space=pltpu.SMEM)
VMEM = pl.BlockSpec(memory_space=pltpu.VMEM)
HBM = pl.BlockSpec(memory_space=pltpu.HBM)


def call(kernel, name, out_shape, in_specs, out_specs, scratch=(), mib=8):
    return pl.pallas_call(
        kernel,
        out_shape=out_shape,
        in_specs=in_specs,
        out_specs=out_specs,
        scratch_shapes=scratch,
        compiler_params=pltpu.CompilerParams(vmem_limit_bytes=mib * 2**20),
        cost_estimate=pl.CostEstimate(flops=1, transcendentals=0, bytes_accessed=1),
        name=name,
    )


def lanczos_tables():
    out_pos = np.arange(TILE)[None, :, None]
    src_pos = np.arange(TILE + 6)[None, None, :] - 3.0
    frac = np.arange(SHIFTS)[:, None, None] / SHIFTS
    dist = src_pos - out_pos - frac
    kernel = np.where(np.abs(dist) < 3.0, np.sinc(dist) * np.sinc(dist / 3.0), 0.0)
    kernel = kernel / np.sum(kernel, axis=2, keepdims=True)
    along_rows = np.zeros((SHIFTS + 1, TILE, FRAME), np.float32)
    along_rows[:SHIFTS, :, : TILE + 6] = kernel
    along_cols = np.zeros((SHIFTS, 2 * TILE, TILE), np.float32)
    along_cols[:, LEAD : LEAD + TILE + 6] = kernel.transpose(0, 2, 1)
    return along_rows.astype(bf16), along_cols.astype(bf16)


def banded(taps, shape, base):
    diff = lax.broadcasted_iota(i32, shape, 0) - lax.broadcasted_iota(i32, shape, 1) + base
    total = jnp.zeros(shape, f32)
    for k in range(KTAPS):
        total = jnp.where(diff == k, taps[:, k : k + 1], total)
    return total


def columns_kernel(taps_hbm, patch_hbm, cell_hbm, img_hbm, out_ref, info_ref, taps_ref, patch_ref, cell_ref, img_ref, sems):
    small = [
        pltpu.make_async_copy(src.at[0], dst, sems.at[n])
        for n, (src, dst) in enumerate(((taps_hbm, taps_ref), (patch_hbm, patch_ref), (cell_hbm, cell_ref)))
    ]
    quarter = COLS // 4
    parts = []
    for n in range(4):
        at = slice(n * quarter, (n + 1) * quarter)
        parts.append(pltpu.make_async_copy(img_hbm.at[0, :, at], img_ref.at[:, at], sems.at[3 + n]))
    for copy in small + parts:
        copy.start()
    for copy in small:
        copy.wait()
    over_cols = banded(taps_ref[...].astype(f32)[1:2], (2 * TILE, TILE), 0)
    lane = lax.broadcasted_iota(i32, (TILE, TILE), 1)
    first = jnp.where(lane >= EDGE, over_cols[TILE:], 0.0).astype(bf16)
    last = jnp.where(lane < EDGE, over_cols[:TILE], 0.0).astype(bf16)
    over_cols = over_cols.astype(bf16)
    owner = patch_ref[...]
    cell = cell_ref[...]
    row0 = 2 * (lax.axis_index("y") * 4 + lax.axis_index("x"))
    down = (owner >> 2) * 8 + (cell >> 3) - lax.broadcasted_iota(i32, owner.shape, 0) - row0
    right = (owner & 3) * 8 + (cell & 7) - lax.broadcasted_iota(i32, owner.shape, 1)
    for n, offset in enumerate((down, right)):
        most = jnp.max(jnp.where(owner >= 0, offset.astype(f32), -8.0)).astype(i32)
        info_ref[n] = jnp.where(most > -8, jnp.clip(most, -2, 2), 0)
    for b in range(BLOCKS):
        if b % 8 == 0 and b < BLOCKS - 1:
            parts[b // 8].wait()
        if b == 0:
            window, weights = img_ref[:, :TILE], first
        elif b == BLOCKS - 1:
            window, weights = img_ref[:, COLS - TILE :], last
        else:
            window, weights = img_ref[:, (b - 1) * TILE : (b + 1) * TILE], over_cols
        out_ref[:, b * TILE : (b + 1) * TILE] = jnp.dot(window, weights, preferred_element_type=f32).astype(bf16)


def rows_kernel(taps_ref, outer_ref, inner_ref, passed_ref, out_ref, window_ref, edge_ref):
    patch = lax.axis_index("y") * 4 + lax.axis_index("x")
    taps = taps_ref[0].astype(f32)
    over_cols = banded(taps[1:2], (2 * TILE, TILE), 0).astype(bf16)
    halo = 2 * HALO
    for odd, top_ref, bot_ref in ((0, outer_ref, inner_ref), (1, inner_ref, outer_ref)):

        @pl.when((patch & 1) == odd)
        def _(top_ref=top_ref, bot_ref=bot_ref):
            for b in range(BLOCKS):
                for side in range(2):
                    k = b - 1 + side
                    for n, ref in enumerate((top_ref, bot_ref)):
                        rows = jnp.zeros((HALO, TILE), bf16)
                        if 0 <= k < BLOCKS - 1:
                            rows = ref[:, k * TILE : (k + 1) * TILE]
                        first = b * halo + n * HALO
                        window_ref[first : first + HALO, side * TILE : (side + 1) * TILE] = rows

    lane = lax.broadcasted_iota(i32, (halo, TILE), 1)
    for part in range(3):
        each = BLOCKS // 3
        got = jnp.dot(
            window_ref[part * each * halo : (part + 1) * each * halo], over_cols, preferred_element_type=f32
        )
        for n in range(each):
            b = part * each + n
            rows = got[n * halo : (n + 1) * halo]
            if b == 0:
                rows = jnp.where(lane >= EDGE, rows, 0.0)
            if b == BLOCKS - 1:
                rows = jnp.where(lane < EDGE, rows, 0.0)
            edge_ref[:, b * TILE : (b + 1) * TILE] = rows.astype(bf16)
    shape = (FRAME, WINDOW)
    row = lax.broadcasted_iota(i32, shape, 0)
    base = jnp.zeros(shape, f32)
    step = lax.broadcasted_iota(i32, shape, 1) - row - 7
    for k in range(KTAPS):
        base = jnp.where(step == k, taps[0:1, k : k + 1], base)
    low = jnp.where(patch == 0, 3, 0)
    high = jnp.where(patch == 15, 130, 133)
    over_rows = (
        jnp.where((row >= low) & (row <= 133), base, 0.0).astype(bf16),
        jnp.where(row <= high, base, 0.0).astype(bf16),
    )
    for n in range(BLOCKS // 3):
        at = slice(n * 3 * TILE, (n + 1) * 3 * TILE)
        upper = jnp.concatenate([edge_ref[:HALO, at], passed_ref[:FRAME, at]], axis=0)
        lower = jnp.concatenate([passed_ref[BAND - FRAME :, at], edge_ref[HALO:, at]], axis=0)
        for r, window in enumerate((upper, lower)):
            out_ref[r, :, at] = jnp.dot(over_rows[r], window, preferred_element_type=f32).astype(bf16)


def warp_kernel(hops, info_ref, patch_ref, class_ref, weight_ref, rows_ref, cols_ref, in_ref, *refs):
    out_refs, half_ref = refs[:-1], refs[-1]
    core = lax.axis_index("core")
    line = lax.broadcasted_iota(i32, (32, TILE), 0)
    weight = jnp.full((32, TILE), weight_ref[0], f32)
    high = weight.astype(bf16).astype(f32)
    mid = (weight - high).astype(bf16).astype(f32)
    low = weight - high - mid
    parts = jnp.where(line < 8, high, jnp.where(line < 16, mid, low))
    down = info_ref[0].astype(f32)
    plan = []
    for n, out_ref in enumerate(out_refs):
        dest = (lax.axis_index("x") + hops[n // 2]) & 3
        half = core if n % 2 == 0 else 1 - core
        marks = jnp.zeros((32, TILE), f32)
        for slot in range(HALF_TILES):
            r, w = divmod(slot, 4)
            col = dest * 8 + half * 4 + w - info_ref[1]
            inside = (col >= 0) & (col < 32)
            col = jnp.clip(col, 0, 31)
            there = inside & (patch_ref[0, r, col] >= 0)
            plan.append((out_ref, slot, r, col, jnp.where(there, class_ref[0, 0, r, col], SHIFTS)))
            marks = jnp.where((line & 7) == slot, jnp.where(there, 1.0, 0.0), marks)
        out_ref[HALF_TILES * TILE :, :] = jnp.where(line < 24, marks * parts, down).astype(bf16)
    for n, (out_ref, slot, r, col, picked) in enumerate(plan):
        tile = in_ref[r, :, pl.ds(pl.multiple_of(col * TILE, TILE), 2 * TILE)]
        half_ref[n] = jnp.dot(tile, cols_ref[class_ref[0, 1, r, col]], preferred_element_type=f32).astype(bf16)
    for n, (out_ref, slot, r, col, picked) in enumerate(plan):
        out_ref[slot * TILE : (slot + 1) * TILE, :] = jnp.dot(
            rows_ref[picked], half_ref[n], preferred_element_type=f32
        ).astype(bf16)


def encode(cells, weights, out_ref, start):
    line = lax.broadcasted_iota(i32, (16, TILE), 0)
    notes = jnp.zeros((16, TILE), f32)
    for w in range(4):
        cell = cells[w]
        most = jnp.max(jnp.max(jnp.abs(cell), axis=0, keepdims=True), axis=1, keepdims=True)
        level = jnp.ceil(jnp.log(jnp.maximum(most, 1e-33)) * (128.0 / math.log(2.0)))
        code = jnp.floor(cell * (TOP_CODE * jnp.exp(level * (-math.log(2.0) / 128.0))) + 0.5)
        out_ref[start + w * TILE : start + (w + 1) * TILE, :] = code.astype(i32).astype(i16)
        whole = jnp.floor(weights[w : w + 1] * 128.0)
        rest = jnp.floor((weights[w : w + 1] * 128.0 - whole) * 32767.0 + 0.5)
        notes = jnp.where(line == w, level, notes)
        notes = jnp.where(line == 4 + w, whole, notes)
        notes = jnp.where(line == 8 + w, rest, notes)
    out_ref[start + 4 * TILE : start + CELLROW, :] = notes.astype(i32).astype(i16)


def decode(in_ref, start):
    notes = in_ref[start + 4 * TILE : start + CELLROW, :].astype(i32).astype(f32)
    cells = []
    for w in range(4):
        scale = jnp.exp(notes[w : w + 1] * (math.log(2.0) / 128.0)) * (1.0 / TOP_CODE)
        code = in_ref[start + w * TILE : start + (w + 1) * TILE, :].astype(i32).astype(f32)
        cells.append(code * scale)
    return cells, (notes[4:8] + notes[8:12] * (1.0 / 32767.0)) * (1.0 / 128.0)


def held(ref, at):
    cells = [ref[at, w * TILE : (w + 1) * TILE, :] for w in range(4)]
    return cells, ref[at, 4 * TILE : 4 * TILE + 4, :]


def added(*parts):
    cells = [sum(p[0][w] for p in parts[1:]) + parts[0][0][w] for w in range(4)]
    return cells, sum(p[1] for p in parts[1:]) + parts[0][1]


def spread(piece, rows_ref, where):
    notes = piece[HALF_TILES * TILE :, :].astype(f32)
    weights = notes[0:8] + notes[8:16] + notes[16:24]
    down = jnp.max(notes[24:32]).astype(i32)
    for r in range(2):
        at = where(r, r + down)
        for w in range(4):
            slot = r * 4 + w
            tile = piece[slot * TILE : (slot + 1) * TILE, :].astype(f32)
            rows_ref[at, w * TILE : (w + 1) * TILE, :] += weights[slot : slot + 1] * tile
        rows_ref[at, 4 * TILE : 4 * TILE + 4, :] += weights[r * 4 : r * 4 + 4]


def spill_kernel(hops, *refs):
    pieces, out_ref, rows_ref = refs[:4], refs[4], refs[5]
    x = lax.axis_index("x")
    rows_ref[...] = jnp.zeros(rows_ref.shape, f32)
    for n, hop in enumerate(sorted(set(hops))):
        mine = [i for i in range(4) if hops[i] == hop]
        band = (x + 4 - hop) & 3

        def where(r, row, band=band):
            slot = jnp.where(band == 0, row + 2, row - 2)
            return jnp.where((slot >= 0) & (slot < 2), slot, 2 + r)

        @pl.when((x == mine[0]) | (x == mine[1]))
        def _(n=n, where=where):
            for piece in pieces[2 * n : 2 * n + 2]:
                spread(piece, rows_ref, where)

    for r in range(2):
        encode(*held(rows_ref, r), out_ref, r * CELLROW)


def place_kernel(*refs):
    pieces, main_ref, rows_ref = refs[:8], refs[8], refs[9]
    rows_ref[...] = jnp.zeros(rows_ref.shape, f32)
    for n, piece in enumerate(pieces):
        band = (lax.axis_index("x") + 4 - n % 4) & 3
        spread(piece, rows_ref, lambda r, row: 2 * band + row + 2)
    main_ref[...] = rows_ref[2:10]


def merge_kernel(in_ref, *refs):
    spills, main_ref, outs = refs[:2], refs[2], refs[3:]
    main_ref[...] = in_ref[...]
    for n, ref in enumerate(spills):
        first = jnp.where((lax.axis_index("x") & 1) == n, 0, 6)
        for r in range(2):
            cells, weights = added(held(main_ref, first + r), decode(ref, r * CELLROW))
            for w in range(4):
                main_ref[first + r, w * TILE : (w + 1) * TILE, :] = cells[w]
            main_ref[first + r, 4 * TILE : 4 * TILE + 4, :] = weights
    z = lax.axis_index("z")
    for ahead, out_ref in zip(FIRST, outs):
        encode(*held(main_ref, (z + 8 + ahead) & 7), out_ref, 0)


def step_kernel(ahead, main_ref, in_ref, out_ref):
    at = (lax.axis_index("z") + 8 + ahead) & 7
    encode(*added(held(main_ref, at), decode(in_ref, 0)), out_ref, 0)


def finish_kernel(main_ref, *refs):
    ins, (coadd_ref, cover_ref) = refs[:-2], refs[-2:]
    z = lax.axis_index("z")
    cells, weights = added(held(main_ref, z), *[decode(ref, 0) for ref in ins])
    lane = lax.broadcasted_iota(i32, (1, TILE), 1)
    cover = jnp.zeros((1, TILE), f32)
    for w in range(4):
        coadd_ref[0, w] = cells[w] / jnp.maximum(weights[w : w + 1], 1.0)
        cover = jnp.where(lane == w, weights[w : w + 1], cover)
    cover_ref[...] = cover[:, :4]


def local(images, psf_taps, exposure_weights, dest_patch, dest_cell, shift_class):
    shape = jax.ShapeDtypeStruct
    edge = (BAND - HALO) * (lax.axis_index("x") & 1)
    outer = lax.dynamic_slice_in_dim(images[0], edge, HALO)
    inner = lax.dynamic_slice_in_dim(images[0], BAND - HALO - edge, HALO)
    outer = lax.ppermute(outer, ("y", "x"), [p for i in range(1, 14, 2) for p in ((i, i + 1), (i + 1, i))])
    inner = lax.ppermute(inner, ("y", "x"), [p for i in range(0, 15, 2) for p in ((i, i + 1), (i + 1, i))])
    rows, cols = (jnp.asarray(t) for t in lanczos_tables())
    passed, info = call(
        columns_kernel,
        "columns",
        (shape((BAND, BLOCKS * TILE), bf16), shape((2,), i32)),
        [HBM] * 4,
        (VMEM, SMEM),
        [
            pltpu.VMEM((2, KTAPS), bf16),
            pltpu.VMEM((2, COLS // TILE), i32),
            pltpu.VMEM((2, COLS // TILE), i32),
            pltpu.VMEM((BAND, COLS), bf16),
            pltpu.SemaphoreType.DMA((7,)),
        ],
    )(*(pltpu.with_memory_space_constraint(a, pltpu.HBM) for a in (psf_taps, dest_patch, dest_cell, images)))
    matched = call(
        rows_kernel,
        "rows",
        shape((2, FRAME, BLOCKS * TILE), bf16),
        [VMEM] * 4,
        VMEM,
        [pltpu.VMEM((BLOCKS * 2 * HALO, 2 * TILE), bf16), pltpu.VMEM((2 * HALO, BLOCKS * TILE), bf16)],
    )(psf_taps, outer, inner, passed)
    piece = shape((PIECE, TILE), bf16)
    own = [None] * 4
    sib = [None] * 4
    for hops in HOPS:
        outs = call(
            lambda *refs, hops=hops: warp_kernel(hops, *refs),
            "warp_" + "".join(str(h) for h in hops),
            (piece,) * (2 * len(hops)),
            [SMEM] * 4 + [VMEM] * 3,
            (VMEM,) * (2 * len(hops)),
            [pltpu.VMEM((2 * HALF_TILES * len(hops), FRAME, TILE), bf16)],
        )(info, dest_patch, shift_class, exposure_weights, rows, cols, matched)
        for n, hop in enumerate(hops):
            own[hop] = outs[2 * n]
            if hop:
                own[hop] = lax.ppermute(own[hop], "x", [(i, (i + hop) % 4) for i in range(4)])
            sib[hop] = lax.ppermute(
                outs[2 * n + 1],
                ("core", "x"),
                [(c * 4 + i, (1 - c) * 4 + (i + hop) % 4) for c in range(2) for i in range(4)],
            )
    held_rows = shape((8, CELLROW, TILE), f32)
    spill = shape((2 * CELLROW, TILE), i16)
    coded = shape((CELLROW, TILE), i16)
    spills = []
    for n, hops in enumerate(((1, 1, 3, 3), (0, 2, 2, 0))):
        out = call(
            lambda *refs, hops=hops: spill_kernel(hops, *refs),
            f"spill_{n}",
            spill,
            [VMEM] * 4,
            VMEM,
            [pltpu.VMEM((4, CELLROW, TILE), f32)],
        )(*(piece for hop in sorted(set(hops)) for piece in (own[hop], sib[hop])))
        lower = [(4 * i + x, 4 * i + 4 + x) for i in range(3) for x in range(4) if x % 2 == n]
        upper = [(4 * i + 4 + x, 4 * i + x) for i in range(3) for x in range(4) if x % 2 != n]
        spills.append(lax.ppermute(out, ("y", "x"), lower + upper))
    main = call(place_kernel, "place", held_rows, [VMEM] * 8, VMEM, [pltpu.VMEM((12, CELLROW, TILE), f32)])(*own, *sib)
    main, *first = call(
        merge_kernel, "merge", (held_rows,) + (coded,) * len(FIRST), [VMEM] * 3, (VMEM,) * (1 + len(FIRST))
    )(main, *spills)

    def along_z(block, hops):
        return lax.ppermute(block, "z", [(i, (i + hops) % 8) for i in range(8)])

    up, dn = first[:2]
    for s in range(CHAIN - 1, -1, -1):
        up, dn = along_z(up, 1), along_z(dn, -1)
        if s:
            up = call(lambda *refs, s=s: step_kernel(s, *refs), f"up_{s}", coded, [VMEM] * 2, VMEM)(main, up)
            dn = call(lambda *refs, s=s: step_kernel(-s, *refs), f"down_{s}", coded, [VMEM] * 2, VMEM)(main, dn)
    far = [along_z(block, ahead) for ahead, block in zip(FIRST[2:], first[2:])]
    return call(
        finish_kernel,
        "finish",
        (shape((1, 4, TILE, TILE), f32), shape((1, 4), f32)),
        [VMEM] * (3 + len(far)),
        (VMEM, VMEM),
    )(main, up, dn, *far)


def solution(mesh):
    split = Mesh(mesh.devices.reshape(8, 2, 4, 4), ("z", "core", "y", "x"))
    visit = ("z", "core")
    patch = ("y", "x")
    placed = (
        P(visit, patch, None),
        P(visit, None, None),
        P(visit),
        P(visit, patch, None),
        P(visit, patch, None),
        P(visit, None, patch, None),
    )
    return jax.shard_map(
        local,
        mesh=split,
        in_specs=placed,
        out_specs=(P(patch, visit, None, None), P(patch, visit)),
        check_vma=False,
    )
```

```python
import math

import jax
import jax.numpy as jnp
import numpy as np
from jax import lax
from jax.experimental import pallas as pl
from jax.experimental.pallas import tpu as pltpu
from jax.sharding import Mesh, PartitionSpec as P

TILE = 128
KTAPS = 13
SHIFTS = 8
HALO = 16
BAND = 256
COLS = 4096
BLOCKS = COLS // TILE + 1
EDGE = 122
FRAME = 144
WINDOW = FRAME + 16
LEAD = 119
HALF_TILES = 8
PIECE = HALF_TILES * TILE + 32
CELLROW = 4 * TILE + 16
TOP_CODE = 32000.0
HOPS = ((1, 3), (2, 0))
LATE = 1
CHAIN = 3
f32 = jnp.float32
bf16 = jnp.bfloat16
i16 = jnp.int16
i32 = jnp.int32
SMEM = pl.BlockSpec(memory_space=pltpu.SMEM)
VMEM = pl.BlockSpec(memory_space=pltpu.VMEM)
HBM = pl.BlockSpec(memory_space=pltpu.HBM)


def call(kernel, name, out_shape, in_specs, out_specs, scratch=(), mib=8):
    return pl.pallas_call(
        kernel,
        out_shape=out_shape,
        in_specs=in_specs,
        out_specs=out_specs,
        scratch_shapes=scratch,
        compiler_params=pltpu.CompilerParams(vmem_limit_bytes=mib * 2**20),
        cost_estimate=pl.CostEstimate(flops=1, transcendentals=0, bytes_accessed=1),
        name=name,
    )


def lanczos_tables():
    out_pos = np.arange(TILE)[None, :, None]
    src_pos = np.arange(TILE + 6)[None, None, :] - 3.0
    frac = np.arange(SHIFTS)[:, None, None] / SHIFTS
    dist = src_pos - out_pos - frac
    kernel = np.where(np.abs(dist) < 3.0, np.sinc(dist) * np.sinc(dist / 3.0), 0.0)
    kernel = kernel / np.sum(kernel, axis=2, keepdims=True)
    along_rows = np.zeros((SHIFTS + 1, TILE, FRAME), np.float32)
    along_rows[:SHIFTS, :, : TILE + 6] = kernel
    along_cols = np.zeros((SHIFTS, 2 * TILE, TILE), np.float32)
    along_cols[:, LEAD : LEAD + TILE + 6] = kernel.transpose(0, 2, 1)
    return along_rows.astype(bf16), along_cols.astype(bf16)


def banded(taps, shape, base):
    diff = lax.broadcasted_iota(i32, shape, 0) - lax.broadcasted_iota(i32, shape, 1) + base
    total = jnp.zeros(shape, f32)
    for k in range(KTAPS):
        total = jnp.where(diff == k, taps[:, k : k + 1], total)
    return total


def columns_kernel(taps_hbm, patch_hbm, cell_hbm, img_hbm, out_ref, info_ref, taps_ref, patch_ref, cell_ref, img_ref, sems):
    small = [
        pltpu.make_async_copy(src.at[0], dst, sems.at[n])
        for n, (src, dst) in enumerate(((taps_hbm, taps_ref), (patch_hbm, patch_ref), (cell_hbm, cell_ref)))
    ]
    quarter = COLS // 4
    parts = []
    for n in range(4):
        at = slice(n * quarter, (n + 1) * quarter)
        parts.append(pltpu.make_async_copy(img_hbm.at[0, :, at], img_ref.at[:, at], sems.at[3 + n]))
    for copy in small + parts:
        copy.start()
    for copy in small:
        copy.wait()
    over_cols = banded(taps_ref[...].astype(f32)[1:2], (2 * TILE, TILE), 0)
    lane = lax.broadcasted_iota(i32, (TILE, TILE), 1)
    first = jnp.where(lane >= EDGE, over_cols[TILE:], 0.0).astype(bf16)
    last = jnp.where(lane < EDGE, over_cols[:TILE], 0.0).astype(bf16)
    over_cols = over_cols.astype(bf16)
    owner = patch_ref[...]
    cell = cell_ref[...]
    row0 = 2 * (lax.axis_index("y") * 4 + lax.axis_index("x"))
    down = (owner >> 2) * 8 + (cell >> 3) - lax.broadcasted_iota(i32, owner.shape, 0) - row0
    right = (owner & 3) * 8 + (cell & 7) - lax.broadcasted_iota(i32, owner.shape, 1)
    for n, offset in enumerate((down, right)):
        most = jnp.max(jnp.where(owner >= 0, offset.astype(f32), -8.0)).astype(i32)
        info_ref[n] = jnp.where(most > -8, jnp.clip(most, -2, 2), 0)
    for b in range(BLOCKS):
        if b % 8 == 0 and b < BLOCKS - 1:
            parts[b // 8].wait()
        if b == 0:
            window, weights = img_ref[:, :TILE], first
        elif b == BLOCKS - 1:
            window, weights = img_ref[:, COLS - TILE :], last
        else:
            window, weights = img_ref[:, (b - 1) * TILE : (b + 1) * TILE], over_cols
        out_ref[:, b * TILE : (b + 1) * TILE] = jnp.dot(window, weights, preferred_element_type=f32).astype(bf16)


def rows_kernel(taps_ref, outer_ref, inner_ref, passed_ref, out_ref, window_ref, edge_ref):
    patch = lax.axis_index("y") * 4 + lax.axis_index("x")
    taps = taps_ref[0].astype(f32)
    over_cols = banded(taps[1:2], (2 * TILE, TILE), 0).astype(bf16)
    halo = 2 * HALO
    for odd, top_ref, bot_ref in ((0, outer_ref, inner_ref), (1, inner_ref, outer_ref)):

        @pl.when((patch & 1) == odd)
        def _(top_ref=top_ref, bot_ref=bot_ref):
            for b in range(BLOCKS):
                for side in range(2):
                    k = b - 1 + side
                    for n, ref in enumerate((top_ref, bot_ref)):
                        rows = jnp.zeros((HALO, TILE), bf16)
                        if 0 <= k < BLOCKS - 1:
                            rows = ref[:, k * TILE : (k + 1) * TILE]
                        first = b * halo + n * HALO
                        window_ref[first : first + HALO, side * TILE : (side + 1) * TILE] = rows

    lane = lax.broadcasted_iota(i32, (halo, TILE), 1)
    for part in range(3):
        each = BLOCKS // 3
        got = jnp.dot(
            window_ref[part * each * halo : (part + 1) * each * halo], over_cols, preferred_element_type=f32
        )
        for n in range(each):
            b = part * each + n
            rows = got[n * halo : (n + 1) * halo]
            if b == 0:
                rows = jnp.where(lane >= EDGE, rows, 0.0)
            if b == BLOCKS - 1:
                rows = jnp.where(lane < EDGE, rows, 0.0)
            edge_ref[:, b * TILE : (b + 1) * TILE] = rows.astype(bf16)
    shape = (FRAME, WINDOW)
    row = lax.broadcasted_iota(i32, shape, 0)
    base = jnp.zeros(shape, f32)
    step = lax.broadcasted_iota(i32, shape, 1) - row - 7
    for k in range(KTAPS):
        base = jnp.where(step == k, taps[0:1, k : k + 1], base)
    low = jnp.where(patch == 0, 3, 0)
    high = jnp.where(patch == 15, 130, 133)
    over_rows = (
        jnp.where((row >= low) & (row <= 133), base, 0.0).astype(bf16),
        jnp.where(row <= high, base, 0.0).astype(bf16),
    )
    for n in range(BLOCKS // 3):
        at = slice(n * 3 * TILE, (n + 1) * 3 * TILE)
        upper = jnp.concatenate([edge_ref[:HALO, at], passed_ref[:FRAME, at]], axis=0)
        lower = jnp.concatenate([passed_ref[BAND - FRAME :, at], edge_ref[HALO:, at]], axis=0)
        for r, window in enumerate((upper, lower)):
            out_ref[r, :, at] = jnp.dot(over_rows[r], window, preferred_element_type=f32).astype(bf16)


def warp_kernel(hops, info_ref, patch_ref, class_ref, weight_ref, rows_ref, cols_ref, in_ref, *refs):
    out_refs, half_ref = refs[:-1], refs[-1]
    core = lax.axis_index("core")
    line = lax.broadcasted_iota(i32, (32, TILE), 0)
    weight = jnp.full((32, TILE), weight_ref[0], f32)
    high = weight.astype(bf16).astype(f32)
    mid = (weight - high).astype(bf16).astype(f32)
    low = weight - high - mid
    parts = jnp.where(line < 8, high, jnp.where(line < 16, mid, low))
    down = info_ref[0].astype(f32)
    plan = []
    for n, out_ref in enumerate(out_refs):
        dest = (lax.axis_index("x") + hops[n // 2]) & 3
        half = core if n % 2 == 0 else 1 - core
        marks = jnp.zeros((32, TILE), f32)
        for slot in range(HALF_TILES):
            r, w = divmod(slot, 4)
            col = dest * 8 + half * 4 + w - info_ref[1]
            inside = (col >= 0) & (col < 32)
            col = jnp.clip(col, 0, 31)
            there = inside & (patch_ref[0, r, col] >= 0)
            plan.append((out_ref, slot, r, col, jnp.where(there, class_ref[0, 0, r, col], SHIFTS)))
            marks = jnp.where((line & 7) == slot, jnp.where(there, 1.0, 0.0), marks)
        out_ref[HALF_TILES * TILE :, :] = jnp.where(line < 24, marks * parts, down).astype(bf16)
    for n, (out_ref, slot, r, col, picked) in enumerate(plan):
        tile = in_ref[r, :, pl.ds(pl.multiple_of(col * TILE, TILE), 2 * TILE)]
        half_ref[n] = jnp.dot(tile, cols_ref[class_ref[0, 1, r, col]], preferred_element_type=f32).astype(bf16)
    for n, (out_ref, slot, r, col, picked) in enumerate(plan):
        out_ref[slot * TILE : (slot + 1) * TILE, :] = jnp.dot(
            rows_ref[picked], half_ref[n], preferred_element_type=f32
        ).astype(bf16)


def encode(cells, weights, out_ref, start):
    line = lax.broadcasted_iota(i32, (16, TILE), 0)
    notes = jnp.zeros((16, TILE), f32)
    for w in range(4):
        cell = cells[w]
        most = jnp.max(jnp.max(jnp.abs(cell), axis=0, keepdims=True), axis=1, keepdims=True)
        level = jnp.ceil(jnp.log(jnp.maximum(most, 1e-33)) * (128.0 / math.log(2.0)))
        code = jnp.floor(cell * (TOP_CODE * jnp.exp(level * (-math.log(2.0) / 128.0))) + 0.5)
        out_ref[start + w * TILE : start + (w + 1) * TILE, :] = code.astype(i32).astype(i16)
        whole = jnp.floor(weights[w : w + 1] * 128.0)
        rest = jnp.floor((weights[w : w + 1] * 128.0 - whole) * 32767.0 + 0.5)
        notes = jnp.where(line == w, level, notes)
        notes = jnp.where(line == 4 + w, whole, notes)
        notes = jnp.where(line == 8 + w, rest, notes)
    out_ref[start + 4 * TILE : start + CELLROW, :] = notes.astype(i32).astype(i16)


def decode(in_ref, start):
    notes = in_ref[start + 4 * TILE : start + CELLROW, :].astype(i32).astype(f32)
    cells = []
    for w in range(4):
        scale = jnp.exp(notes[w : w + 1] * (math.log(2.0) / 128.0)) * (1.0 / TOP_CODE)
        code = in_ref[start + w * TILE : start + (w + 1) * TILE, :].astype(i32).astype(f32)
        cells.append(code * scale)
    return cells, (notes[4:8] + notes[8:12] * (1.0 / 32767.0)) * (1.0 / 128.0)


def held(ref, at):
    cells = [ref[at, w * TILE : (w + 1) * TILE, :] for w in range(4)]
    return cells, ref[at, 4 * TILE : 4 * TILE + 4, :]


def added(*parts):
    cells = [sum(p[0][w] for p in parts[1:]) + parts[0][0][w] for w in range(4)]
    return cells, sum(p[1] for p in parts[1:]) + parts[0][1]


def spread(piece, rows_ref, where):
    notes = piece[HALF_TILES * TILE :, :].astype(f32)
    weights = notes[0:8] + notes[8:16] + notes[16:24]
    down = jnp.max(notes[24:32]).astype(i32)
    for r in range(2):
        at = where(r, r + down)
        for w in range(4):
            slot = r * 4 + w
            tile = piece[slot * TILE : (slot + 1) * TILE, :].astype(f32)
            rows_ref[at, w * TILE : (w + 1) * TILE, :] += weights[slot : slot + 1] * tile
        rows_ref[at, 4 * TILE : 4 * TILE + 4, :] += weights[r * 4 : r * 4 + 4]


def spill_kernel(hops, *refs):
    pieces, out_ref, rows_ref = refs[:4], refs[4], refs[5]
    x = lax.axis_index("x")
    rows_ref[...] = jnp.zeros(rows_ref.shape, f32)
    for n, hop in enumerate(sorted(set(hops))):
        mine = [i for i in range(4) if hops[i] == hop]
        band = (x + 4 - hop) & 3

        def where(r, row, band=band):
            slot = jnp.where(band == 0, row + 2, row - 2)
            return jnp.where((slot >= 0) & (slot < 2), slot, 2 + r)

        @pl.when((x == mine[0]) | (x == mine[1]))
        def _(n=n, where=where):
            for piece in pieces[2 * n : 2 * n + 2]:
                spread(piece, rows_ref, where)

    for r in range(2):
        encode(*held(rows_ref, r), out_ref, r * CELLROW)


def place_kernel(*refs):
    pieces, main_ref, rows_ref = refs[:8], refs[8], refs[9]
    rows_ref[...] = jnp.zeros(rows_ref.shape, f32)
    for n, piece in enumerate(pieces):
        band = (lax.axis_index("x") + 4 - n % 4) & 3
        spread(piece, rows_ref, lambda r, row: 2 * band + row + 2)
    main_ref[...] = rows_ref[2:10]


def merge_kernel(in_ref, *refs):
    spills, main_ref, outs = refs[:2], refs[2], refs[3:]
    main_ref[...] = in_ref[...]
    for n, ref in enumerate(spills):
        first = jnp.where((lax.axis_index("x") & 1) == n, 0, 6)
        for r in range(2):
            cells, weights = added(held(main_ref, first + r), decode(ref, r * CELLROW))
            for w in range(4):
                main_ref[first + r, w * TILE : (w + 1) * TILE, :] = cells[w]
            main_ref[first + r, 4 * TILE : 4 * TILE + 4, :] = weights
    z = lax.axis_index("z")
    for ahead, out_ref in zip((upward(CHAIN), -upward(CHAIN), 4), outs):
        encode(*held(main_ref, (z + 8 + ahead) & 7), out_ref, 0)


def upward(by):
    return by - 2 * by * (lax.axis_index("z") & 1)


def step_kernel(ahead, main_ref, in_ref, *refs):
    out_ref = refs[-1]
    at = (lax.axis_index("z") + 8 + upward(ahead)) & 7
    encode(*added(held(main_ref, at), decode(in_ref, 0)), out_ref, 0)


def fold_kernel(main_ref, far_ref, out_ref):
    cells, weights = added(held(main_ref, lax.axis_index("z")), decode(far_ref, 0))
    for w in range(4):
        out_ref[0, w * TILE : (w + 1) * TILE, :] = cells[w]
    out_ref[0, 4 * TILE : 4 * TILE + 4, :] = weights


def finish_kernel(own_ref, *refs):
    ins, (coadd_ref, cover_ref) = refs[:-2], refs[-2:]
    cells, weights = added(held(own_ref, 0), *[decode(ref, 0) for ref in ins])
    lane = lax.broadcasted_iota(i32, (1, TILE), 1)
    cover = jnp.zeros((1, TILE), f32)
    for w in range(4):
        coadd_ref[0, w] = cells[w] / jnp.maximum(weights[w : w + 1], 1.0)
        cover = jnp.where(lane == w, weights[w : w + 1], cover)
    cover_ref[...] = cover[:, :4]


def local(images, psf_taps, exposure_weights, dest_patch, dest_cell, shift_class):
    shape = jax.ShapeDtypeStruct
    edge = (BAND - HALO) * (lax.axis_index("x") & 1)
    outer = lax.dynamic_slice_in_dim(images[0], edge, HALO)
    inner = lax.dynamic_slice_in_dim(images[0], BAND - HALO - edge, HALO)
    outer = lax.ppermute(outer, ("y", "x"), [p for i in range(1, 14, 2) for p in ((i, i + 1), (i + 1, i))])
    inner = lax.ppermute(inner, ("y", "x"), [p for i in range(0, 15, 2) for p in ((i, i + 1), (i + 1, i))])
    rows, cols = (jnp.asarray(t) for t in lanczos_tables())
    passed, info = call(
        columns_kernel,
        "columns",
        (shape((BAND, BLOCKS * TILE), bf16), shape((2,), i32)),
        [HBM] * 4,
        (VMEM, SMEM),
        [
            pltpu.VMEM((2, KTAPS), bf16),
            pltpu.VMEM((2, COLS // TILE), i32),
            pltpu.VMEM((2, COLS // TILE), i32),
            pltpu.VMEM((BAND, COLS), bf16),
            pltpu.SemaphoreType.DMA((7,)),
        ],
    )(*(pltpu.with_memory_space_constraint(a, pltpu.HBM) for a in (psf_taps, dest_patch, dest_cell, images)))
    matched = call(
        rows_kernel,
        "rows",
        shape((2, FRAME, BLOCKS * TILE), bf16),
        [VMEM] * 4,
        VMEM,
        [pltpu.VMEM((BLOCKS * 2 * HALO, 2 * TILE), bf16), pltpu.VMEM((2 * HALO, BLOCKS * TILE), bf16)],
    )(psf_taps, outer, inner, passed)
    piece = shape((PIECE, TILE), bf16)
    own = [None] * 4
    sib = [None] * 4
    for hops in HOPS:
        outs = call(
            lambda *refs, hops=hops: warp_kernel(hops, *refs),
            "warp_" + "".join(str(h) for h in hops),
            (piece,) * (2 * len(hops)),
            [SMEM] * 4 + [VMEM] * 3,
            (VMEM,) * (2 * len(hops)),
            [pltpu.VMEM((2 * HALF_TILES * len(hops), FRAME, TILE), bf16)],
        )(info, dest_patch, shift_class, exposure_weights, rows, cols, matched)
        for n, hop in enumerate(hops):
            own[hop] = outs[2 * n]
            if hop:
                own[hop] = lax.ppermute(own[hop], "x", [(i, (i + hop) % 4) for i in range(4)])
            sib[hop] = lax.ppermute(
                outs[2 * n + 1],
                ("core", "x"),
                [(c * 4 + i, (1 - c) * 4 + (i + hop) % 4) for c in range(2) for i in range(4)],
            )
    held_rows = shape((8, CELLROW, TILE), f32)
    spill = shape((2 * CELLROW, TILE), i16)
    coded = shape((CELLROW, TILE), i16)
    spills = []
    for n, hops in enumerate(((1, 1, 3, 3), (0, 2, 2, 0))):
        out = call(
            lambda *refs, hops=hops: spill_kernel(hops, *refs),
            f"spill_{n}",
            spill,
            [VMEM] * 4,
            VMEM,
            [pltpu.VMEM((4, CELLROW, TILE), f32)],
        )(*(piece for hop in sorted(set(hops)) for piece in (own[hop], sib[hop])))
        lower = [(4 * i + x, 4 * i + 4 + x) for i in range(3) for x in range(4) if x % 2 == n]
        upper = [(4 * i + 4 + x, 4 * i + x) for i in range(3) for x in range(4) if x % 2 != n]
        spills.append(lax.ppermute(out, ("y", "x"), lower + upper))
    main = call(place_kernel, "place", held_rows, [VMEM] * 8, VMEM, [pltpu.VMEM((12, CELLROW, TILE), f32)])(*own, *sib)
    main, one, two, far = call(
        merge_kernel, "merge", (held_rows,) + (coded,) * 3, [VMEM] * 3, (VMEM,) * 4
    )(main, *spills)

    pairs = [[p for i in range(n, 8, 2) for p in ((i, (i + 1) % 8), ((i + 1) % 8, i))] for n in range(2)]
    far = lax.ppermute(far, "z", [(i, (i + 4) % 8) for i in range(8)])
    mine = call(fold_kernel, "fold", shape((1, CELLROW, TILE), f32), [VMEM] * 2, VMEM)(main, far)
    for s in range(CHAIN - 1, -1, -1):
        got_one, got_two = lax.ppermute(one, "z", pairs[0]), lax.ppermute(two, "z", pairs[1])
        one, two = got_two, got_one
        if s:
            after = (mine,) if s == LATE else ()
            ins = [VMEM] * (2 + len(after))
            one = call(lambda *refs, s=s: step_kernel(s, *refs), f"one_{s}", coded, ins, VMEM)(main, got_two, *after)
            two = call(lambda *refs, s=s: step_kernel(-s, *refs), f"two_{s}", coded, ins, VMEM)(main, got_one, *after)
    return call(
        finish_kernel,
        "finish",
        (shape((1, 4, TILE, TILE), f32), shape((1, 4), f32)),
        [VMEM] * 3,
        (VMEM, VMEM),
    )(mine, one, two)


def solution(mesh):
    split = Mesh(mesh.devices.reshape(8, 2, 4, 4), ("z", "core", "y", "x"))
    visit = ("z", "core")
    patch = ("y", "x")
    placed = (
        P(visit, patch, None),
        P(visit, None, None),
        P(visit),
        P(visit, patch, None),
        P(visit, patch, None),
        P(visit, None, patch, None),
    )
    return jax.shard_map(
        local,
        mesh=split,
        in_specs=placed,
        out_specs=(P(patch, visit, None, None), P(patch, visit)),
        check_vma=False,
    )
```

```python
import math

import jax
import jax.numpy as jnp
import numpy as np
from jax import lax
from jax.experimental import pallas as pl
from jax.experimental.pallas import tpu as pltpu
from jax.sharding import Mesh, PartitionSpec as P

TILE = 128
KTAPS = 13
SHIFTS = 8
HALO = 16
BAND = 256
COLS = 4096
BLOCKS = COLS // TILE + 1
EDGE = 122
FRAME = 144
WINDOW = FRAME + 16
LEAD = 119
HALF_TILES = 8
PIECE = HALF_TILES * TILE + 32
CELLROW = 4 * TILE + 16
TOP_CODE = 32000.0
SENDS = (((2, 0), (2, 1)), ((1, 0), (3, 0), (1, 1), (3, 1), (0, 0), (0, 1)))
LATE = 1
CHAIN = 3
f32 = jnp.float32
bf16 = jnp.bfloat16
i16 = jnp.int16
i32 = jnp.int32
SMEM = pl.BlockSpec(memory_space=pltpu.SMEM)
VMEM = pl.BlockSpec(memory_space=pltpu.VMEM)
HBM = pl.BlockSpec(memory_space=pltpu.HBM)


def call(kernel, name, out_shape, in_specs, out_specs, scratch=(), mib=8):
    return pl.pallas_call(
        kernel,
        out_shape=out_shape,
        in_specs=in_specs,
        out_specs=out_specs,
        scratch_shapes=scratch,
        compiler_params=pltpu.CompilerParams(vmem_limit_bytes=mib * 2**20),
        cost_estimate=pl.CostEstimate(flops=1, transcendentals=0, bytes_accessed=1),
        name=name,
    )


def lanczos_tables():
    out_pos = np.arange(TILE)[None, :, None]
    src_pos = np.arange(TILE + 6)[None, None, :] - 3.0
    frac = np.arange(SHIFTS)[:, None, None] / SHIFTS
    dist = src_pos - out_pos - frac
    kernel = np.where(np.abs(dist) < 3.0, np.sinc(dist) * np.sinc(dist / 3.0), 0.0)
    kernel = kernel / np.sum(kernel, axis=2, keepdims=True)
    along_rows = np.zeros((SHIFTS + 1, TILE, FRAME), np.float32)
    along_rows[:SHIFTS, :, : TILE + 6] = kernel
    along_cols = np.zeros((SHIFTS, 2 * TILE, TILE), np.float32)
    along_cols[:, LEAD : LEAD + TILE + 6] = kernel.transpose(0, 2, 1)
    return along_rows.astype(bf16), along_cols.astype(bf16)


def banded(taps, shape, base):
    diff = lax.broadcasted_iota(i32, shape, 0) - lax.broadcasted_iota(i32, shape, 1) + base
    total = jnp.zeros(shape, f32)
    for k in range(KTAPS):
        total = jnp.where(diff == k, taps[:, k : k + 1], total)
    return total


def columns_kernel(taps_hbm, patch_hbm, cell_hbm, img_hbm, out_ref, info_ref, taps_ref, patch_ref, cell_ref, img_ref, sems):
    small = [
        pltpu.make_async_copy(src.at[0], dst, sems.at[n])
        for n, (src, dst) in enumerate(((taps_hbm, taps_ref), (patch_hbm, patch_ref), (cell_hbm, cell_ref)))
    ]
    quarter = COLS // 4
    parts = []
    for n in range(4):
        at = slice(n * quarter, (n + 1) * quarter)
        parts.append(pltpu.make_async_copy(img_hbm.at[0, :, at], img_ref.at[:, at], sems.at[3 + n]))
    for copy in small + parts:
        copy.start()
    for copy in small:
        copy.wait()
    over_cols = banded(taps_ref[...].astype(f32)[1:2], (2 * TILE, TILE), 0)
    lane = lax.broadcasted_iota(i32, (TILE, TILE), 1)
    first = jnp.where(lane >= EDGE, over_cols[TILE:], 0.0).astype(bf16)
    last = jnp.where(lane < EDGE, over_cols[:TILE], 0.0).astype(bf16)
    over_cols = over_cols.astype(bf16)
    owner = patch_ref[...]
    cell = cell_ref[...]
    row0 = 2 * (lax.axis_index("y") * 4 + lax.axis_index("x"))
    down = (owner >> 2) * 8 + (cell >> 3) - lax.broadcasted_iota(i32, owner.shape, 0) - row0
    right = (owner & 3) * 8 + (cell & 7) - lax.broadcasted_iota(i32, owner.shape, 1)
    for n, offset in enumerate((down, right)):
        most = jnp.max(jnp.where(owner >= 0, offset.astype(f32), -8.0)).astype(i32)
        info_ref[n] = jnp.where(most > -8, jnp.clip(most, -2, 2), 0)
    for b in range(BLOCKS):
        if b % 8 == 0 and b < BLOCKS - 1:
            parts[b // 8].wait()
        if b == 0:
            window, weights = img_ref[:, :TILE], first
        elif b == BLOCKS - 1:
            window, weights = img_ref[:, COLS - TILE :], last
        else:
            window, weights = img_ref[:, (b - 1) * TILE : (b + 1) * TILE], over_cols
        out_ref[:, b * TILE : (b + 1) * TILE] = jnp.dot(window, weights, preferred_element_type=f32).astype(bf16)


def rows_kernel(taps_ref, outer_ref, inner_ref, passed_ref, out_ref, window_ref, edge_ref):
    patch = lax.axis_index("y") * 4 + lax.axis_index("x")
    taps = taps_ref[0].astype(f32)
    over_cols = banded(taps[1:2], (2 * TILE, TILE), 0).astype(bf16)
    halo = 2 * HALO
    for odd, top_ref, bot_ref in ((0, outer_ref, inner_ref), (1, inner_ref, outer_ref)):

        @pl.when((patch & 1) == odd)
        def _(top_ref=top_ref, bot_ref=bot_ref):
            for b in range(BLOCKS):
                for side in range(2):
                    k = b - 1 + side
                    for n, ref in enumerate((top_ref, bot_ref)):
                        rows = jnp.zeros((HALO, TILE), bf16)
                        if 0 <= k < BLOCKS - 1:
                            rows = ref[:, k * TILE : (k + 1) * TILE]
                        first = b * halo + n * HALO
                        window_ref[first : first + HALO, side * TILE : (side + 1) * TILE] = rows

    lane = lax.broadcasted_iota(i32, (halo, TILE), 1)
    for part in range(3):
        each = BLOCKS // 3
        got = jnp.dot(
            window_ref[part * each * halo : (part + 1) * each * halo], over_cols, preferred_element_type=f32
        )
        for n in range(each):
            b = part * each + n
            rows = got[n * halo : (n + 1) * halo]
            if b == 0:
                rows = jnp.where(lane >= EDGE, rows, 0.0)
            if b == BLOCKS - 1:
                rows = jnp.where(lane < EDGE, rows, 0.0)
            edge_ref[:, b * TILE : (b + 1) * TILE] = rows.astype(bf16)
    shape = (FRAME, WINDOW)
    row = lax.broadcasted_iota(i32, shape, 0)
    base = jnp.zeros(shape, f32)
    step = lax.broadcasted_iota(i32, shape, 1) - row - 7
    for k in range(KTAPS):
        base = jnp.where(step == k, taps[0:1, k : k + 1], base)
    low = jnp.where(patch == 0, 3, 0)
    high = jnp.where(patch == 15, 130, 133)
    over_rows = (
        jnp.where((row >= low) & (row <= 133), base, 0.0).astype(bf16),
        jnp.where(row <= high, base, 0.0).astype(bf16),
    )
    for n in range(BLOCKS // 3):
        at = slice(n * 3 * TILE, (n + 1) * 3 * TILE)
        upper = jnp.concatenate([edge_ref[:HALO, at], passed_ref[:FRAME, at]], axis=0)
        lower = jnp.concatenate([passed_ref[BAND - FRAME :, at], edge_ref[HALO:, at]], axis=0)
        for r, window in enumerate((upper, lower)):
            out_ref[r, :, at] = jnp.dot(over_rows[r], window, preferred_element_type=f32).astype(bf16)


def warp_kernel(sends, info_ref, patch_ref, class_ref, weight_ref, rows_ref, cols_ref, in_ref, *refs):
    out_refs, half_ref = refs[:-1], refs[-1]
    core = lax.axis_index("core")
    line = lax.broadcasted_iota(i32, (32, TILE), 0)
    weight = jnp.full((32, TILE), weight_ref[0], f32)
    high = weight.astype(bf16).astype(f32)
    mid = (weight - high).astype(bf16).astype(f32)
    low = weight - high - mid
    parts = jnp.where(line < 8, high, jnp.where(line < 16, mid, low))
    down = info_ref[0].astype(f32)
    plan = []
    for n, out_ref in enumerate(out_refs):
        dest = (lax.axis_index("x") + sends[n][0]) & 3
        half = 1 - core if sends[n][1] else core
        marks = jnp.zeros((32, TILE), f32)
        for slot in range(HALF_TILES):
            r, w = divmod(slot, 4)
            col = dest * 8 + half * 4 + w - info_ref[1]
            inside = (col >= 0) & (col < 32)
            col = jnp.clip(col, 0, 31)
            there = inside & (patch_ref[0, r, col] >= 0)
            plan.append((out_ref, slot, r, col, jnp.where(there, class_ref[0, 0, r, col], SHIFTS)))
            marks = jnp.where((line & 7) == slot, jnp.where(there, 1.0, 0.0), marks)
        out_ref[HALF_TILES * TILE :, :] = jnp.where(line < 24, marks * parts, down).astype(bf16)
    for n, (out_ref, slot, r, col, picked) in enumerate(plan):
        tile = in_ref[r, :, pl.ds(pl.multiple_of(col * TILE, TILE), 2 * TILE)]
        half_ref[n] = jnp.dot(tile, cols_ref[class_ref[0, 1, r, col]], preferred_element_type=f32).astype(bf16)
    for n, (out_ref, slot, r, col, picked) in enumerate(plan):
        out_ref[slot * TILE : (slot + 1) * TILE, :] = jnp.dot(
            rows_ref[picked], half_ref[n], preferred_element_type=f32
        ).astype(bf16)


def encode(cells, weights, out_ref, start):
    line = lax.broadcasted_iota(i32, (16, TILE), 0)
    notes = jnp.zeros((16, TILE), f32)
    for w in range(4):
        cell = cells[w]
        most = jnp.max(jnp.max(jnp.abs(cell), axis=0, keepdims=True), axis=1, keepdims=True)
        level = jnp.ceil(jnp.log(jnp.maximum(most, 1e-33)) * (128.0 / math.log(2.0)))
        code = jnp.floor(cell * (TOP_CODE * jnp.exp(level * (-math.log(2.0) / 128.0))) + 0.5)
        out_ref[start + w * TILE : start + (w + 1) * TILE, :] = code.astype(i32).astype(i16)
        whole = jnp.floor(weights[w : w + 1] * 128.0)
        rest = jnp.floor((weights[w : w + 1] * 128.0 - whole) * 32767.0 + 0.5)
        notes = jnp.where(line == w, level, notes)
        notes = jnp.where(line == 4 + w, whole, notes)
        notes = jnp.where(line == 8 + w, rest, notes)
    out_ref[start + 4 * TILE : start + CELLROW, :] = notes.astype(i32).astype(i16)


def decode(in_ref, start):
    notes = in_ref[start + 4 * TILE : start + CELLROW, :].astype(i32).astype(f32)
    cells = []
    for w in range(4):
        scale = jnp.exp(notes[w : w + 1] * (math.log(2.0) / 128.0)) * (1.0 / TOP_CODE)
        code = in_ref[start + w * TILE : start + (w + 1) * TILE, :].astype(i32).astype(f32)
        cells.append(code * scale)
    return cells, (notes[4:8] + notes[8:12] * (1.0 / 32767.0)) * (1.0 / 128.0)


def held(ref, at):
    cells = [ref[at, w * TILE : (w + 1) * TILE, :] for w in range(4)]
    return cells, ref[at, 4 * TILE : 4 * TILE + 4, :]


def added(*parts):
    cells = [sum(p[0][w] for p in parts[1:]) + parts[0][0][w] for w in range(4)]
    return cells, sum(p[1] for p in parts[1:]) + parts[0][1]


def spread(piece, rows_ref, where):
    notes = piece[HALF_TILES * TILE :, :].astype(f32)
    weights = notes[0:8] + notes[8:16] + notes[16:24]
    down = jnp.max(notes[24:32]).astype(i32)
    for r in range(2):
        at = where(r, r + down)
        for w in range(4):
            slot = r * 4 + w
            tile = piece[slot * TILE : (slot + 1) * TILE, :].astype(f32)
            rows_ref[at, w * TILE : (w + 1) * TILE, :] += weights[slot : slot + 1] * tile
        rows_ref[at, 4 * TILE : 4 * TILE + 4, :] += weights[r * 4 : r * 4 + 4]


def spill_kernel(hops, *refs):
    pieces, out_ref, rows_ref = refs[:4], refs[4], refs[5]
    x = lax.axis_index("x")
    rows_ref[...] = jnp.zeros(rows_ref.shape, f32)
    for n, hop in enumerate(sorted(set(hops))):
        mine = [i for i in range(4) if hops[i] == hop]
        band = (x + 4 - hop) & 3

        def where(r, row, band=band):
            slot = jnp.where(band == 0, row + 2, row - 2)
            return jnp.where((slot >= 0) & (slot < 2), slot, 2 + r)

        @pl.when((x == mine[0]) | (x == mine[1]))
        def _(n=n, where=where):
            for piece in pieces[2 * n : 2 * n + 2]:
                spread(piece, rows_ref, where)

    for r in range(2):
        encode(*held(rows_ref, r), out_ref, r * CELLROW)


def place_kernel(*refs):
    pieces, main_ref, rows_ref = refs[:8], refs[8], refs[9]
    rows_ref[...] = jnp.zeros(rows_ref.shape, f32)
    for n, piece in enumerate(pieces):
        band = (lax.axis_index("x") + 4 - n % 4) & 3
        spread(piece, rows_ref, lambda r, row: 2 * band + row + 2)
    main_ref[...] = rows_ref[2:10]


def merge_kernel(in_ref, *refs):
    spills, main_ref, outs = refs[:2], refs[2], refs[3:]
    main_ref[...] = in_ref[...]
    for n, ref in enumerate(spills):
        first = jnp.where((lax.axis_index("x") & 1) == n, 0, 6)
        for r in range(2):
            cells, weights = added(held(main_ref, first + r), decode(ref, r * CELLROW))
            for w in range(4):
                main_ref[first + r, w * TILE : (w + 1) * TILE, :] = cells[w]
            main_ref[first + r, 4 * TILE : 4 * TILE + 4, :] = weights
    z = lax.axis_index("z")
    for ahead, out_ref in zip((upward(CHAIN), -upward(CHAIN), 4), outs):
        encode(*held(main_ref, (z + 8 + ahead) & 7), out_ref, 0)


def upward(by):
    return by - 2 * by * (lax.axis_index("z") & 1)


def step_kernel(ahead, main_ref, in_ref, *refs):
    out_ref = refs[-1]
    at = (lax.axis_index("z") + 8 + upward(ahead)) & 7
    encode(*added(held(main_ref, at), decode(in_ref, 0)), out_ref, 0)


def fold_kernel(main_ref, far_ref, out_ref):
    cells, weights = added(held(main_ref, lax.axis_index("z")), decode(far_ref, 0))
    for w in range(4):
        out_ref[0, w * TILE : (w + 1) * TILE, :] = cells[w]
    out_ref[0, 4 * TILE : 4 * TILE + 4, :] = weights


def finish_kernel(own_ref, *refs):
    ins, (coadd_ref, cover_ref) = refs[:-2], refs[-2:]
    cells, weights = added(held(own_ref, 0), *[decode(ref, 0) for ref in ins])
    lane = lax.broadcasted_iota(i32, (1, TILE), 1)
    cover = jnp.zeros((1, TILE), f32)
    for w in range(4):
        coadd_ref[0, w] = cells[w] / jnp.maximum(weights[w : w + 1], 1.0)
        cover = jnp.where(lane == w, weights[w : w + 1], cover)
    cover_ref[...] = cover[:, :4]


def local(images, psf_taps, exposure_weights, dest_patch, dest_cell, shift_class):
    shape = jax.ShapeDtypeStruct
    edge = (BAND - HALO) * (lax.axis_index("x") & 1)
    outer = lax.dynamic_slice_in_dim(images[0], edge, HALO)
    inner = lax.dynamic_slice_in_dim(images[0], BAND - HALO - edge, HALO)
    outer = lax.ppermute(outer, ("y", "x"), [p for i in range(1, 14, 2) for p in ((i, i + 1), (i + 1, i))])
    inner = lax.ppermute(inner, ("y", "x"), [p for i in range(0, 15, 2) for p in ((i, i + 1), (i + 1, i))])
    rows, cols = (jnp.asarray(t) for t in lanczos_tables())
    passed, info = call(
        columns_kernel,
        "columns",
        (shape((BAND, BLOCKS * TILE), bf16), shape((2,), i32)),
        [HBM] * 4,
        (VMEM, SMEM),
        [
            pltpu.VMEM((2, KTAPS), bf16),
            pltpu.VMEM((2, COLS // TILE), i32),
            pltpu.VMEM((2, COLS // TILE), i32),
            pltpu.VMEM((BAND, COLS), bf16),
            pltpu.SemaphoreType.DMA((7,)),
        ],
    )(*(pltpu.with_memory_space_constraint(a, pltpu.HBM) for a in (psf_taps, dest_patch, dest_cell, images)))
    matched = call(
        rows_kernel,
        "rows",
        shape((2, FRAME, BLOCKS * TILE), bf16),
        [VMEM] * 4,
        VMEM,
        [pltpu.VMEM((BLOCKS * 2 * HALO, 2 * TILE), bf16), pltpu.VMEM((2 * HALO, BLOCKS * TILE), bf16)],
    )(psf_taps, outer, inner, passed)
    piece = shape((PIECE, TILE), bf16)
    own = [None] * 4
    sib = [None] * 4
    for sends in SENDS:
        outs = call(
            lambda *refs, sends=sends: warp_kernel(sends, *refs),
            f"warp_{len(sends)}",
            (piece,) * len(sends),
            [SMEM] * 4 + [VMEM] * 3,
            (VMEM,) * len(sends),
            [pltpu.VMEM((HALF_TILES * len(sends), FRAME, TILE), bf16)],
        )(info, dest_patch, shift_class, exposure_weights, rows, cols, matched)
        for (hop, swap), out in zip(sends, outs):
            if hop or swap:
                out = lax.ppermute(
                    out, ("core", "x"), [(c * 4 + i, (c ^ swap) * 4 + (i + hop) % 4) for c in range(2) for i in range(4)]
                )
            (sib if swap else own)[hop] = out
    held_rows = shape((8, CELLROW, TILE), f32)
    spill = shape((2 * CELLROW, TILE), i16)
    coded = shape((CELLROW, TILE), i16)
    spills = []
    for n, hops in enumerate(((1, 1, 3, 3), (0, 2, 2, 0))):
        out = call(
            lambda *refs, hops=hops: spill_kernel(hops, *refs),
            f"spill_{n}",
            spill,
            [VMEM] * 4,
            VMEM,
            [pltpu.VMEM((4, CELLROW, TILE), f32)],
        )(*(piece for hop in sorted(set(hops)) for piece in (own[hop], sib[hop])))
        lower = [(4 * i + x, 4 * i + 4 + x) for i in range(3) for x in range(4) if x % 2 == n]
        upper = [(4 * i + 4 + x, 4 * i + x) for i in range(3) for x in range(4) if x % 2 != n]
        spills.append(lax.ppermute(out, ("y", "x"), lower + upper))
    main = call(place_kernel, "place", held_rows, [VMEM] * 8, VMEM, [pltpu.VMEM((12, CELLROW, TILE), f32)])(*own, *sib)
    main, one, two, far = call(
        merge_kernel, "merge", (held_rows,) + (coded,) * 3, [VMEM] * 3, (VMEM,) * 4
    )(main, *spills)

    pairs = [[p for i in range(n, 8, 2) for p in ((i, (i + 1) % 8), ((i + 1) % 8, i))] for n in range(2)]
    far = lax.ppermute(far, "z", [(i, (i + 4) % 8) for i in range(8)])
    mine = call(fold_kernel, "fold", shape((1, CELLROW, TILE), f32), [VMEM] * 2, VMEM)(main, far)
    for s in range(CHAIN - 1, -1, -1):
        got_one, got_two = lax.ppermute(one, "z", pairs[0]), lax.ppermute(two, "z", pairs[1])
        one, two = got_two, got_one
        if s:
            after = (mine,) if s == LATE else ()
            ins = [VMEM] * (2 + len(after))
            one = call(lambda *refs, s=s: step_kernel(s, *refs), f"one_{s}", coded, ins, VMEM)(main, got_two, *after)
            two = call(lambda *refs, s=s: step_kernel(-s, *refs), f"two_{s}", coded, ins, VMEM)(main, got_one, *after)
    return call(
        finish_kernel,
        "finish",
        (shape((1, 4, TILE, TILE), f32), shape((1, 4), f32)),
        [VMEM] * 3,
        (VMEM, VMEM),
    )(mine, one, two)


def solution(mesh):
    split = Mesh(mesh.devices.reshape(8, 2, 4, 4), ("z", "core", "y", "x"))
    visit = ("z", "core")
    patch = ("y", "x")
    placed = (
        P(visit, patch, None),
        P(visit, None, None),
        P(visit),
        P(visit, patch, None),
        P(visit, patch, None),
        P(visit, None, patch, None),
    )
    return jax.shard_map(
        local,
        mesh=split,
        in_specs=placed,
        out_specs=(P(patch, visit, None, None), P(patch, visit)),
        check_vma=False,
    )
```

```python
import math

import jax
import jax.numpy as jnp
import numpy as np
from jax import lax
from jax.experimental import pallas as pl
from jax.experimental.pallas import tpu as pltpu
from jax.sharding import Mesh, PartitionSpec as P

TILE = 128
KTAPS = 13
SHIFTS = 8
HALO = 16
BAND = 256
COLS = 4096
BLOCKS = COLS // TILE + 1
EDGE = 122
FRAME = 144
WINDOW = FRAME + 16
LEAD = 119
HALF_TILES = 8
PIECE = HALF_TILES * TILE + 32
CELLROW = 4 * TILE + 16
TOP_CODE = 32000.0
SENDS = (((2, 0), (2, 1)), ((1, 0), (3, 0), (1, 1), (3, 1), (0, 0), (0, 1)))
LATE = 1
CHAIN = 3
f32 = jnp.float32
bf16 = jnp.bfloat16
i16 = jnp.int16
i32 = jnp.int32
SMEM = pl.BlockSpec(memory_space=pltpu.SMEM)
VMEM = pl.BlockSpec(memory_space=pltpu.VMEM)
HBM = pl.BlockSpec(memory_space=pltpu.HBM)


def call(kernel, name, out_shape, in_specs, out_specs, scratch=(), mib=8):
    return pl.pallas_call(
        kernel,
        out_shape=out_shape,
        in_specs=in_specs,
        out_specs=out_specs,
        scratch_shapes=scratch,
        compiler_params=pltpu.CompilerParams(vmem_limit_bytes=mib * 2**20),
        cost_estimate=pl.CostEstimate(flops=1, transcendentals=0, bytes_accessed=1),
        name=name,
    )


def lanczos_tables():
    out_pos = np.arange(TILE)[None, :, None]
    src_pos = np.arange(TILE + 6)[None, None, :] - 3.0
    frac = np.arange(SHIFTS)[:, None, None] / SHIFTS
    dist = src_pos - out_pos - frac
    kernel = np.where(np.abs(dist) < 3.0, np.sinc(dist) * np.sinc(dist / 3.0), 0.0)
    kernel = kernel / np.sum(kernel, axis=2, keepdims=True)
    along_rows = np.zeros((SHIFTS + 1, TILE, FRAME), np.float32)
    along_rows[:SHIFTS, :, : TILE + 6] = kernel
    along_cols = np.zeros((SHIFTS, 2 * TILE, TILE), np.float32)
    along_cols[:, LEAD : LEAD + TILE + 6] = kernel.transpose(0, 2, 1)
    return along_rows.astype(bf16), along_cols.astype(bf16)


def banded(taps, shape, base):
    diff = lax.broadcasted_iota(i32, shape, 0) - lax.broadcasted_iota(i32, shape, 1) + base
    total = jnp.zeros(shape, f32)
    for k in range(KTAPS):
        total = jnp.where(diff == k, taps[:, k : k + 1], total)
    return total


def columns_kernel(taps_hbm, patch_hbm, cell_hbm, img_hbm, out_ref, info_ref, taps_ref, patch_ref, cell_ref, img_ref, sems):
    small = [
        pltpu.make_async_copy(src.at[0], dst, sems.at[n])
        for n, (src, dst) in enumerate(((taps_hbm, taps_ref), (patch_hbm, patch_ref), (cell_hbm, cell_ref)))
    ]
    quarter = COLS // 4
    parts = []
    for n in range(4):
        at = slice(n * quarter, (n + 1) * quarter)
        parts.append(pltpu.make_async_copy(img_hbm.at[0, :, at], img_ref.at[:, at], sems.at[3 + n]))
    for copy in small + parts:
        copy.start()
    for copy in small:
        copy.wait()
    over_cols = banded(taps_ref[...].astype(f32)[1:2], (2 * TILE, TILE), 0)
    lane = lax.broadcasted_iota(i32, (TILE, TILE), 1)
    first = jnp.where(lane >= EDGE, over_cols[TILE:], 0.0).astype(bf16)
    last = jnp.where(lane < EDGE, over_cols[:TILE], 0.0).astype(bf16)
    over_cols = over_cols.astype(bf16)
    owner = patch_ref[...]
    cell = cell_ref[...]
    row0 = 2 * (lax.axis_index("y") * 4 + lax.axis_index("x"))
    down = (owner >> 2) * 8 + (cell >> 3) - lax.broadcasted_iota(i32, owner.shape, 0) - row0
    right = (owner & 3) * 8 + (cell & 7) - lax.broadcasted_iota(i32, owner.shape, 1)
    for n, offset in enumerate((down, right)):
        most = jnp.max(jnp.where(owner >= 0, offset.astype(f32), -8.0)).astype(i32)
        info_ref[n] = jnp.where(most > -8, jnp.clip(most, -2, 2), 0)
    for b in range(BLOCKS):
        if b % 8 == 0 and b < BLOCKS - 1:
            parts[b // 8].wait()
        if b == 0:
            window, weights = img_ref[:, :TILE], first
        elif b == BLOCKS - 1:
            window, weights = img_ref[:, COLS - TILE :], last
        else:
            window, weights = img_ref[:, (b - 1) * TILE : (b + 1) * TILE], over_cols
        out_ref[:, b * TILE : (b + 1) * TILE] = jnp.dot(window, weights, preferred_element_type=f32).astype(bf16)


def rows_kernel(taps_ref, inner_ref, outer_ref, passed_ref, out_ref, window_ref, edge_ref):
    patch = lax.axis_index("y") * 4 + lax.axis_index("x")
    taps = taps_ref[0].astype(f32)
    over_cols = banded(taps[1:2], (2 * TILE, TILE), 0).astype(bf16)
    halo = 2 * HALO
    for odd, top_ref, bot_ref in ((0, outer_ref, inner_ref), (1, inner_ref, outer_ref)):

        @pl.when((patch & 1) == odd)
        def _(top_ref=top_ref, bot_ref=bot_ref):
            for b in range(BLOCKS):
                for side in range(2):
                    k = b - 1 + side
                    for n, ref in enumerate((top_ref, bot_ref)):
                        rows = jnp.zeros((HALO, TILE), bf16)
                        if 0 <= k < BLOCKS - 1:
                            rows = ref[:, k * TILE : (k + 1) * TILE]
                        first = b * halo + n * HALO
                        window_ref[first : first + HALO, side * TILE : (side + 1) * TILE] = rows

    lane = lax.broadcasted_iota(i32, (halo, TILE), 1)
    for part in range(3):
        each = BLOCKS // 3
        got = jnp.dot(
            window_ref[part * each * halo : (part + 1) * each * halo], over_cols, preferred_element_type=f32
        )
        for n in range(each):
            b = part * each + n
            rows = got[n * halo : (n + 1) * halo]
            if b == 0:
                rows = jnp.where(lane >= EDGE, rows, 0.0)
            if b == BLOCKS - 1:
                rows = jnp.where(lane < EDGE, rows, 0.0)
            edge_ref[:, b * TILE : (b + 1) * TILE] = rows.astype(bf16)
    shape = (FRAME, WINDOW)
    row = lax.broadcasted_iota(i32, shape, 0)
    base = jnp.zeros(shape, f32)
    step = lax.broadcasted_iota(i32, shape, 1) - row - 7
    for k in range(KTAPS):
        base = jnp.where(step == k, taps[0:1, k : k + 1], base)
    low = jnp.where(patch == 0, 3, 0)
    high = jnp.where(patch == 15, 130, 133)
    over_rows = (
        jnp.where((row >= low) & (row <= 133), base, 0.0).astype(bf16),
        jnp.where(row <= high, base, 0.0).astype(bf16),
    )
    for n in range(BLOCKS // 3):
        at = slice(n * 3 * TILE, (n + 1) * 3 * TILE)
        upper = jnp.concatenate([edge_ref[:HALO, at], passed_ref[:FRAME, at]], axis=0)
        lower = jnp.concatenate([passed_ref[BAND - FRAME :, at], edge_ref[HALO:, at]], axis=0)
        for r, window in enumerate((upper, lower)):
            out_ref[r, :, at] = jnp.dot(over_rows[r], window, preferred_element_type=f32).astype(bf16)


def warp_kernel(sends, info_ref, patch_ref, class_ref, weight_ref, rows_ref, cols_ref, in_ref, *refs):
    out_refs, half_ref = refs[:-1], refs[-1]
    core = lax.axis_index("core")
    line = lax.broadcasted_iota(i32, (32, TILE), 0)
    weight = jnp.full((32, TILE), weight_ref[0], f32)
    high = weight.astype(bf16).astype(f32)
    mid = (weight - high).astype(bf16).astype(f32)
    low = weight - high - mid
    parts = jnp.where(line < 8, high, jnp.where(line < 16, mid, low))
    down = info_ref[0].astype(f32)
    plan = []
    for n, out_ref in enumerate(out_refs):
        dest = (lax.axis_index("x") + sends[n][0]) & 3
        half = 1 - core if sends[n][1] else core
        marks = jnp.zeros((32, TILE), f32)
        for slot in range(HALF_TILES):
            r, w = divmod(slot, 4)
            col = dest * 8 + half * 4 + w - info_ref[1]
            inside = (col >= 0) & (col < 32)
            col = jnp.clip(col, 0, 31)
            there = inside & (patch_ref[0, r, col] >= 0)
            plan.append((out_ref, slot, r, col, jnp.where(there, class_ref[0, 0, r, col], SHIFTS)))
            marks = jnp.where((line & 7) == slot, jnp.where(there, 1.0, 0.0), marks)
        out_ref[HALF_TILES * TILE :, :] = jnp.where(line < 24, marks * parts, down).astype(bf16)
    for n, (out_ref, slot, r, col, picked) in enumerate(plan):
        tile = in_ref[r, :, pl.ds(pl.multiple_of(col * TILE, TILE), 2 * TILE)]
        half_ref[n] = jnp.dot(tile, cols_ref[class_ref[0, 1, r, col]], preferred_element_type=f32).astype(bf16)
    for n, (out_ref, slot, r, col, picked) in enumerate(plan):
        out_ref[slot * TILE : (slot + 1) * TILE, :] = jnp.dot(
            rows_ref[picked], half_ref[n], preferred_element_type=f32
        ).astype(bf16)


def encode(cells, weights, out_ref, start):
    line = lax.broadcasted_iota(i32, (16, TILE), 0)
    notes = jnp.zeros((16, TILE), f32)
    for w in range(4):
        cell = cells[w]
        most = jnp.max(jnp.max(jnp.abs(cell), axis=0, keepdims=True), axis=1, keepdims=True)
        level = jnp.ceil(jnp.log(jnp.maximum(most, 1e-33)) * (128.0 / math.log(2.0)))
        code = jnp.floor(cell * (TOP_CODE * jnp.exp(level * (-math.log(2.0) / 128.0))) + 0.5)
        out_ref[start + w * TILE : start + (w + 1) * TILE, :] = code.astype(i32).astype(i16)
        whole = jnp.floor(weights[w : w + 1] * 128.0)
        rest = jnp.floor((weights[w : w + 1] * 128.0 - whole) * 32767.0 + 0.5)
        notes = jnp.where(line == w, level, notes)
        notes = jnp.where(line == 4 + w, whole, notes)
        notes = jnp.where(line == 8 + w, rest, notes)
    out_ref[start + 4 * TILE : start + CELLROW, :] = notes.astype(i32).astype(i16)


def decode(in_ref, start):
    notes = in_ref[start + 4 * TILE : start + CELLROW, :].astype(i32).astype(f32)
    cells = []
    for w in range(4):
        scale = jnp.exp(notes[w : w + 1] * (math.log(2.0) / 128.0)) * (1.0 / TOP_CODE)
        code = in_ref[start + w * TILE : start + (w + 1) * TILE, :].astype(i32).astype(f32)
        cells.append(code * scale)
    return cells, (notes[4:8] + notes[8:12] * (1.0 / 32767.0)) * (1.0 / 128.0)


def held(ref, at):
    cells = [ref[at, w * TILE : (w + 1) * TILE, :] for w in range(4)]
    return cells, ref[at, 4 * TILE : 4 * TILE + 4, :]


def added(*parts):
    cells = [sum(p[0][w] for p in parts[1:]) + parts[0][0][w] for w in range(4)]
    return cells, sum(p[1] for p in parts[1:]) + parts[0][1]


def spread(piece, rows_ref, where):
    notes = piece[HALF_TILES * TILE :, :].astype(f32)
    weights = notes[0:8] + notes[8:16] + notes[16:24]
    down = jnp.max(notes[24:32]).astype(i32)
    for r in range(2):
        at = where(r, r + down)
        for w in range(4):
            slot = r * 4 + w
            tile = piece[slot * TILE : (slot + 1) * TILE, :].astype(f32)
            rows_ref[at, w * TILE : (w + 1) * TILE, :] += weights[slot : slot + 1] * tile
        rows_ref[at, 4 * TILE : 4 * TILE + 4, :] += weights[r * 4 : r * 4 + 4]


def spill_kernel(hops, *refs):
    pieces, out_ref, rows_ref = refs[:4], refs[4], refs[5]
    x = lax.axis_index("x")
    rows_ref[...] = jnp.zeros(rows_ref.shape, f32)
    for n, hop in enumerate(sorted(set(hops))):
        mine = [i for i in range(4) if hops[i] == hop]
        band = (x + 4 - hop) & 3

        def where(r, row, band=band):
            slot = jnp.where(band == 0, row + 2, row - 2)
            return jnp.where((slot >= 0) & (slot < 2), slot, 2 + r)

        @pl.when((x == mine[0]) | (x == mine[1]))
        def _(n=n, where=where):
            for piece in pieces[2 * n : 2 * n + 2]:
                spread(piece, rows_ref, where)

    for r in range(2):
        encode(*held(rows_ref, r), out_ref, r * CELLROW)


def place_kernel(*refs):
    pieces, main_ref, rows_ref = refs[:8], refs[8], refs[9]
    rows_ref[...] = jnp.zeros(rows_ref.shape, f32)
    for n, piece in enumerate(pieces):
        band = (lax.axis_index("x") + 4 - n % 4) & 3
        spread(piece, rows_ref, lambda r, row: 2 * band + row + 2)
    main_ref[...] = rows_ref[2:10]


def merge_kernel(in_ref, *refs):
    spills, main_ref, outs = refs[:2], refs[2], refs[3:]
    main_ref[...] = in_ref[...]
    for n, ref in enumerate(spills):
        first = jnp.where((lax.axis_index("x") & 1) == n, 0, 6)
        for r in range(2):
            cells, weights = added(held(main_ref, first + r), decode(ref, r * CELLROW))
            for w in range(4):
                main_ref[first + r, w * TILE : (w + 1) * TILE, :] = cells[w]
            main_ref[first + r, 4 * TILE : 4 * TILE + 4, :] = weights
    z = lax.axis_index("z")
    for ahead, out_ref in zip((upward(CHAIN), -upward(CHAIN), 4), outs):
        encode(*held(main_ref, (z + 8 + ahead) & 7), out_ref, 0)


def upward(by):
    return by - 2 * by * (lax.axis_index("z") & 1)


def step_kernel(ahead, main_ref, in_ref, *refs):
    out_ref = refs[-1]
    at = (lax.axis_index("z") + 8 + upward(ahead)) & 7
    encode(*added(held(main_ref, at), decode(in_ref, 0)), out_ref, 0)


def fold_kernel(main_ref, far_ref, out_ref):
    cells, weights = added(held(main_ref, lax.axis_index("z")), decode(far_ref, 0))
    for w in range(4):
        out_ref[0, w * TILE : (w + 1) * TILE, :] = cells[w]
    out_ref[0, 4 * TILE : 4 * TILE + 4, :] = weights


def finish_kernel(own_ref, *refs):
    ins, (coadd_ref, cover_ref) = refs[:-2], refs[-2:]
    cells, weights = added(held(own_ref, 0), *[decode(ref, 0) for ref in ins])
    lane = lax.broadcasted_iota(i32, (1, TILE), 1)
    cover = jnp.zeros((1, TILE), f32)
    for w in range(4):
        coadd_ref[0, w] = cells[w] / jnp.maximum(weights[w : w + 1], 1.0)
        cover = jnp.where(lane == w, weights[w : w + 1], cover)
    cover_ref[...] = cover[:, :4]


def local(images, psf_taps, exposure_weights, dest_patch, dest_cell, shift_class):
    shape = jax.ShapeDtypeStruct
    edge = (BAND - HALO) * (lax.axis_index("x") & 1)
    outer = lax.dynamic_slice_in_dim(images[0], edge, HALO)
    inner = lax.dynamic_slice_in_dim(images[0], BAND - HALO - edge, HALO)
    outer = lax.ppermute(outer, ("y", "x"), [p for i in range(1, 14, 2) for p in ((i, i + 1), (i + 1, i))])
    inner = lax.ppermute(inner, ("y", "x"), [p for i in range(0, 15, 2) for p in ((i, i + 1), (i + 1, i))])
    rows, cols = (jnp.asarray(t) for t in lanczos_tables())
    passed, info = call(
        columns_kernel,
        "columns",
        (shape((BAND, BLOCKS * TILE), bf16), shape((2,), i32)),
        [HBM] * 4,
        (VMEM, SMEM),
        [
            pltpu.VMEM((2, KTAPS), bf16),
            pltpu.VMEM((2, COLS // TILE), i32),
            pltpu.VMEM((2, COLS // TILE), i32),
            pltpu.VMEM((BAND, COLS), bf16),
            pltpu.SemaphoreType.DMA((7,)),
        ],
    )(*(pltpu.with_memory_space_constraint(a, pltpu.HBM) for a in (psf_taps, dest_patch, dest_cell, images)))
    matched = call(
        rows_kernel,
        "rows",
        shape((2, FRAME, BLOCKS * TILE), bf16),
        [VMEM] * 4,
        VMEM,
        [pltpu.VMEM((BLOCKS * 2 * HALO, 2 * TILE), bf16), pltpu.VMEM((2 * HALO, BLOCKS * TILE), bf16)],
    )(psf_taps, inner, outer, passed)
    piece = shape((PIECE, TILE), bf16)
    own = [None] * 4
    sib = [None] * 4
    for sends in SENDS:
        outs = call(
            lambda *refs, sends=sends: warp_kernel(sends, *refs),
            f"warp_{len(sends)}",
            (piece,) * len(sends),
            [SMEM] * 4 + [VMEM] * 3,
            (VMEM,) * len(sends),
            [pltpu.VMEM((HALF_TILES * len(sends), FRAME, TILE), bf16)],
        )(info, dest_patch, shift_class, exposure_weights, rows, cols, matched)
        for (hop, swap), out in zip(sends, outs):
            if hop or swap:
                out = lax.ppermute(
                    out, ("core", "x"), [(c * 4 + i, (c ^ swap) * 4 + (i + hop) % 4) for c in range(2) for i in range(4)]
                )
            (sib if swap else own)[hop] = out
    held_rows = shape((8, CELLROW, TILE), f32)
    spill = shape((2 * CELLROW, TILE), i16)
    coded = shape((CELLROW, TILE), i16)
    spills = []
    for n, hops in enumerate(((1, 1, 3, 3), (0, 2, 2, 0))):
        out = call(
            lambda *refs, hops=hops: spill_kernel(hops, *refs),
            f"spill_{n}",
            spill,
            [VMEM] * 4,
            VMEM,
            [pltpu.VMEM((4, CELLROW, TILE), f32)],
        )(*(piece for hop in sorted(set(hops)) for piece in (own[hop], sib[hop])))
        lower = [(4 * i + x, 4 * i + 4 + x) for i in range(3) for x in range(4) if x % 2 == n]
        upper = [(4 * i + 4 + x, 4 * i + x) for i in range(3) for x in range(4) if x % 2 != n]
        spills.append(lax.ppermute(out, ("y", "x"), lower + upper))
    main = call(place_kernel, "place", held_rows, [VMEM] * 8, VMEM, [pltpu.VMEM((12, CELLROW, TILE), f32)])(*own, *sib)
    main, one, two, far = call(
        merge_kernel, "merge", (held_rows,) + (coded,) * 3, [VMEM] * 3, (VMEM,) * 4
    )(main, *spills)

    pairs = [[p for i in range(n, 8, 2) for p in ((i, (i + 1) % 8), ((i + 1) % 8, i))] for n in range(2)]
    far = lax.ppermute(far, "z", [(i, (i + 4) % 8) for i in range(8)])
    mine = call(fold_kernel, "fold", shape((1, CELLROW, TILE), f32), [VMEM] * 2, VMEM)(main, far)
    for s in range(CHAIN - 1, -1, -1):
        got_one, got_two = lax.ppermute(one, "z", pairs[0]), lax.ppermute(two, "z", pairs[1])
        one, two = got_two, got_one
        if s:
            after = (mine,) if s == LATE else ()
            ins = [VMEM] * (2 + len(after))
            one = call(lambda *refs, s=s: step_kernel(s, *refs), f"one_{s}", coded, ins, VMEM)(main, got_two, *after)
            two = call(lambda *refs, s=s: step_kernel(-s, *refs), f"two_{s}", coded, ins, VMEM)(main, got_one, *after)
    return call(
        finish_kernel,
        "finish",
        (shape((1, 4, TILE, TILE), f32), shape((1, 4), f32)),
        [VMEM] * 3,
        (VMEM, VMEM),
    )(mine, one, two)


def solution(mesh):
    split = Mesh(mesh.devices.reshape(8, 2, 4, 4), ("z", "core", "y", "x"))
    visit = ("z", "core")
    patch = ("y", "x")
    placed = (
        P(visit, patch, None),
        P(visit, None, None),
        P(visit),
        P(visit, patch, None),
        P(visit, patch, None),
        P(visit, None, patch, None),
    )
    return jax.shard_map(
        local,
        mesh=split,
        in_specs=placed,
        out_specs=(P(patch, visit, None, None), P(patch, visit)),
        check_vma=False,
    )
```

```python
import math

import jax
import jax.numpy as jnp
import numpy as np
from jax import lax
from jax.experimental import pallas as pl
from jax.experimental.pallas import tpu as pltpu
from jax.sharding import Mesh, PartitionSpec as P

TILE = 128
KTAPS = 13
SHIFTS = 8
HALO = 16
BAND = 256
COLS = 4096
BLOCKS = COLS // TILE + 1
EDGE = 122
FRAME = 144
WINDOW = FRAME + 16
LEAD = 119
HALF_TILES = 8
PIECE = HALF_TILES * TILE + 32
CELLROW = 4 * TILE + 16
TOP_CODE = 32000.0
SENDS = (((2, 0), (2, 1)), ((1, 0), (3, 0), (1, 1), (3, 1), (0, 0), (0, 1)))
LATE = 1
CHAIN = 3
f32 = jnp.float32
bf16 = jnp.bfloat16
i16 = jnp.int16
i32 = jnp.int32
SMEM = pl.BlockSpec(memory_space=pltpu.SMEM)
VMEM = pl.BlockSpec(memory_space=pltpu.VMEM)
HBM = pl.BlockSpec(memory_space=pltpu.HBM)


def call(kernel, name, out_shape, in_specs, out_specs, scratch=(), mib=8):
    return pl.pallas_call(
        kernel,
        out_shape=out_shape,
        in_specs=in_specs,
        out_specs=out_specs,
        scratch_shapes=scratch,
        compiler_params=pltpu.CompilerParams(vmem_limit_bytes=mib * 2**20),
        cost_estimate=pl.CostEstimate(flops=1, transcendentals=0, bytes_accessed=1),
        name=name,
    )


def lanczos_tables():
    out_pos = np.arange(TILE)[None, :, None]
    src_pos = np.arange(TILE + 6)[None, None, :] - 3.0
    frac = np.arange(SHIFTS)[:, None, None] / SHIFTS
    dist = src_pos - out_pos - frac
    kernel = np.where(np.abs(dist) < 3.0, np.sinc(dist) * np.sinc(dist / 3.0), 0.0)
    kernel = kernel / np.sum(kernel, axis=2, keepdims=True)
    along_rows = np.zeros((SHIFTS + 1, TILE, FRAME), np.float32)
    along_rows[:SHIFTS, :, : TILE + 6] = kernel
    along_cols = np.zeros((SHIFTS, 2 * TILE, TILE), np.float32)
    along_cols[:, LEAD : LEAD + TILE + 6] = kernel.transpose(0, 2, 1)
    return along_rows.astype(bf16), along_cols.astype(bf16)


def banded(taps, shape, base):
    diff = lax.broadcasted_iota(i32, shape, 0) - lax.broadcasted_iota(i32, shape, 1) + base
    total = jnp.zeros(shape, f32)
    for k in range(KTAPS):
        total = jnp.where(diff == k, taps[:, k : k + 1], total)
    return total


def columns_kernel(taps_hbm, patch_hbm, cell_hbm, img_hbm, out_ref, info_ref, cols_out, rows_out, taps_ref, patch_ref, cell_ref, img_ref, sems):
    small = [
        pltpu.make_async_copy(src.at[0], dst, sems.at[n])
        for n, (src, dst) in enumerate(((taps_hbm, taps_ref), (patch_hbm, patch_ref), (cell_hbm, cell_ref)))
    ]
    quarter = COLS // 4
    parts = []
    for n in range(4):
        at = slice(n * quarter, (n + 1) * quarter)
        parts.append(pltpu.make_async_copy(img_hbm.at[0, :, at], img_ref.at[:, at], sems.at[3 + n]))
    for copy in small + parts:
        copy.start()
    for copy in small:
        copy.wait()
    over_cols = banded(taps_ref[...].astype(f32)[1:2], (2 * TILE, TILE), 0)
    lane = lax.broadcasted_iota(i32, (TILE, TILE), 1)
    first = jnp.where(lane >= EDGE, over_cols[TILE:], 0.0).astype(bf16)
    last = jnp.where(lane < EDGE, over_cols[:TILE], 0.0).astype(bf16)
    over_cols = over_cols.astype(bf16)
    cols_out[...] = over_cols
    patch = lax.axis_index("y") * 4 + lax.axis_index("x")
    taps = taps_ref[...].astype(f32)
    shape = (FRAME, WINDOW)
    row = lax.broadcasted_iota(i32, shape, 0)
    base = jnp.zeros(shape, f32)
    step = lax.broadcasted_iota(i32, shape, 1) - row - 7
    for k in range(KTAPS):
        base = jnp.where(step == k, taps[0:1, k : k + 1], base)
    low = jnp.where(patch == 0, 3, 0)
    high = jnp.where(patch == 15, 130, 133)
    rows_out[0] = jnp.where((row >= low) & (row <= 133), base, 0.0).astype(bf16)
    rows_out[1] = jnp.where(row <= high, base, 0.0).astype(bf16)
    owner = patch_ref[...]
    cell = cell_ref[...]
    row0 = 2 * (lax.axis_index("y") * 4 + lax.axis_index("x"))
    down = (owner >> 2) * 8 + (cell >> 3) - lax.broadcasted_iota(i32, owner.shape, 0) - row0
    right = (owner & 3) * 8 + (cell & 7) - lax.broadcasted_iota(i32, owner.shape, 1)
    for n, offset in enumerate((down, right)):
        most = jnp.max(jnp.where(owner >= 0, offset.astype(f32), -8.0)).astype(i32)
        info_ref[n] = jnp.where(most > -8, jnp.clip(most, -2, 2), 0)
    for b in range(BLOCKS):
        if b % 8 == 0 and b < BLOCKS - 1:
            parts[b // 8].wait()
        if b == 0:
            window, weights = img_ref[:, :TILE], first
        elif b == BLOCKS - 1:
            window, weights = img_ref[:, COLS - TILE :], last
        else:
            window, weights = img_ref[:, (b - 1) * TILE : (b + 1) * TILE], over_cols
        out_ref[:, b * TILE : (b + 1) * TILE] = jnp.dot(window, weights, preferred_element_type=f32).astype(bf16)


def rows_kernel(cols_ref, rows_ref, inner_ref, outer_ref, passed_ref, out_ref, window_ref, edge_ref):
    patch = lax.axis_index("y") * 4 + lax.axis_index("x")
    over_cols = cols_ref[...]
    halo = 2 * HALO
    for odd, top_ref, bot_ref in ((0, outer_ref, inner_ref), (1, inner_ref, outer_ref)):

        @pl.when((patch & 1) == odd)
        def _(top_ref=top_ref, bot_ref=bot_ref):
            for b in range(BLOCKS):
                for side in range(2):
                    k = b - 1 + side
                    for n, ref in enumerate((top_ref, bot_ref)):
                        rows = jnp.zeros((HALO, TILE), bf16)
                        if 0 <= k < BLOCKS - 1:
                            rows = ref[:, k * TILE : (k + 1) * TILE]
                        first = b * halo + n * HALO
                        window_ref[first : first + HALO, side * TILE : (side + 1) * TILE] = rows

    lane = lax.broadcasted_iota(i32, (halo, TILE), 1)
    for part in range(3):
        each = BLOCKS // 3
        got = jnp.dot(
            window_ref[part * each * halo : (part + 1) * each * halo], over_cols, preferred_element_type=f32
        )
        for n in range(each):
            b = part * each + n
            rows = got[n * halo : (n + 1) * halo]
            if b == 0:
                rows = jnp.where(lane >= EDGE, rows, 0.0)
            if b == BLOCKS - 1:
                rows = jnp.where(lane < EDGE, rows, 0.0)
            edge_ref[:, b * TILE : (b + 1) * TILE] = rows.astype(bf16)
    for n in range(BLOCKS // 3):
        at = slice(n * 3 * TILE, (n + 1) * 3 * TILE)
        upper = jnp.concatenate([edge_ref[:HALO, at], passed_ref[:FRAME, at]], axis=0)
        lower = jnp.concatenate([passed_ref[BAND - FRAME :, at], edge_ref[HALO:, at]], axis=0)
        for r, window in enumerate((upper, lower)):
            out_ref[r, :, at] = jnp.dot(rows_ref[r], window, preferred_element_type=f32).astype(bf16)


def warp_kernel(sends, info_ref, patch_ref, class_ref, weight_ref, rows_ref, cols_ref, in_ref, *refs):
    out_refs, half_ref = refs[:-1], refs[-1]
    core = lax.axis_index("core")
    line = lax.broadcasted_iota(i32, (32, TILE), 0)
    weight = jnp.full((32, TILE), weight_ref[0], f32)
    high = weight.astype(bf16).astype(f32)
    mid = (weight - high).astype(bf16).astype(f32)
    low = weight - high - mid
    parts = jnp.where(line < 8, high, jnp.where(line < 16, mid, low))
    down = info_ref[0].astype(f32)
    plan = []
    for n, out_ref in enumerate(out_refs):
        dest = (lax.axis_index("x") + sends[n][0]) & 3
        half = 1 - core if sends[n][1] else core
        marks = jnp.zeros((32, TILE), f32)
        for slot in range(HALF_TILES):
            r, w = divmod(slot, 4)
            col = dest * 8 + half * 4 + w - info_ref[1]
            inside = (col >= 0) & (col < 32)
            col = jnp.clip(col, 0, 31)
            there = inside & (patch_ref[0, r, col] >= 0)
            plan.append((out_ref, slot, r, col, jnp.where(there, class_ref[0, 0, r, col], SHIFTS)))
            marks = jnp.where((line & 7) == slot, jnp.where(there, 1.0, 0.0), marks)
        out_ref[HALF_TILES * TILE :, :] = jnp.where(line < 24, marks * parts, down).astype(bf16)
    for n, (out_ref, slot, r, col, picked) in enumerate(plan):
        tile = in_ref[r, :, pl.ds(pl.multiple_of(col * TILE, TILE), 2 * TILE)]
        half_ref[n] = jnp.dot(tile, cols_ref[class_ref[0, 1, r, col]], preferred_element_type=f32).astype(bf16)
    for n, (out_ref, slot, r, col, picked) in enumerate(plan):
        out_ref[slot * TILE : (slot + 1) * TILE, :] = jnp.dot(
            rows_ref[picked], half_ref[n], preferred_element_type=f32
        ).astype(bf16)


def encode(cells, weights, out_ref, start):
    line = lax.broadcasted_iota(i32, (16, TILE), 0)
    notes = jnp.zeros((16, TILE), f32)
    for w in range(4):
        cell = cells[w]
        most = jnp.max(jnp.max(jnp.abs(cell), axis=0, keepdims=True), axis=1, keepdims=True)
        level = jnp.ceil(jnp.log(jnp.maximum(most, 1e-33)) * (128.0 / math.log(2.0)))
        code = jnp.floor(cell * (TOP_CODE * jnp.exp(level * (-math.log(2.0) / 128.0))) + 0.5)
        out_ref[start + w * TILE : start + (w + 1) * TILE, :] = code.astype(i32).astype(i16)
        whole = jnp.floor(weights[w : w + 1] * 128.0)
        rest = jnp.floor((weights[w : w + 1] * 128.0 - whole) * 32767.0 + 0.5)
        notes = jnp.where(line == w, level, notes)
        notes = jnp.where(line == 4 + w, whole, notes)
        notes = jnp.where(line == 8 + w, rest, notes)
    out_ref[start + 4 * TILE : start + CELLROW, :] = notes.astype(i32).astype(i16)


def decode(in_ref, start):
    notes = in_ref[start + 4 * TILE : start + CELLROW, :].astype(i32).astype(f32)
    cells = []
    for w in range(4):
        scale = jnp.exp(notes[w : w + 1] * (math.log(2.0) / 128.0)) * (1.0 / TOP_CODE)
        code = in_ref[start + w * TILE : start + (w + 1) * TILE, :].astype(i32).astype(f32)
        cells.append(code * scale)
    return cells, (notes[4:8] + notes[8:12] * (1.0 / 32767.0)) * (1.0 / 128.0)


def held(ref, at):
    cells = [ref[at, w * TILE : (w + 1) * TILE, :] for w in range(4)]
    return cells, ref[at, 4 * TILE : 4 * TILE + 4, :]


def added(*parts):
    cells = [sum(p[0][w] for p in parts[1:]) + parts[0][0][w] for w in range(4)]
    return cells, sum(p[1] for p in parts[1:]) + parts[0][1]


def spread(piece, rows_ref, where):
    notes = piece[HALF_TILES * TILE :, :].astype(f32)
    weights = notes[0:8] + notes[8:16] + notes[16:24]
    down = jnp.max(notes[24:32]).astype(i32)
    for r in range(2):
        at = where(r, r + down)
        for w in range(4):
            slot = r * 4 + w
            tile = piece[slot * TILE : (slot + 1) * TILE, :].astype(f32)
            rows_ref[at, w * TILE : (w + 1) * TILE, :] += weights[slot : slot + 1] * tile
        rows_ref[at, 4 * TILE : 4 * TILE + 4, :] += weights[r * 4 : r * 4 + 4]


def spill_kernel(hops, *refs):
    pieces, out_ref, rows_ref = refs[:4], refs[4], refs[5]
    x = lax.axis_index("x")
    rows_ref[...] = jnp.zeros(rows_ref.shape, f32)
    for n, hop in enumerate(sorted(set(hops))):
        mine = [i for i in range(4) if hops[i] == hop]
        band = (x + 4 - hop) & 3

        def where(r, row, band=band):
            slot = jnp.where(band == 0, row + 2, row - 2)
            return jnp.where((slot >= 0) & (slot < 2), slot, 2 + r)

        @pl.when((x == mine[0]) | (x == mine[1]))
        def _(n=n, where=where):
            for piece in pieces[2 * n : 2 * n + 2]:
                spread(piece, rows_ref, where)

    for r in range(2):
        encode(*held(rows_ref, r), out_ref, r * CELLROW)


def place_kernel(*refs):
    pieces, main_ref, rows_ref = refs[:8], refs[8], refs[9]
    rows_ref[...] = jnp.zeros(rows_ref.shape, f32)
    for n, piece in enumerate(pieces):
        band = (lax.axis_index("x") + 4 - n % 4) & 3
        spread(piece, rows_ref, lambda r, row: 2 * band + row + 2)
    main_ref[...] = rows_ref[2:10]


def merge_kernel(in_ref, *refs):
    spills, main_ref, outs = refs[:2], refs[2], refs[3:]
    main_ref[2:6] = in_ref[2:6]
    for n, ref in enumerate(spills):
        first = jnp.where((lax.axis_index("x") & 1) == n, 0, 6)
        for r in range(2):
            cells, weights = added(held(in_ref, first + r), decode(ref, r * CELLROW))
            for w in range(4):
                main_ref[first + r, w * TILE : (w + 1) * TILE, :] = cells[w]
            main_ref[first + r, 4 * TILE : 4 * TILE + 4, :] = weights
    z = lax.axis_index("z")
    for ahead, out_ref in zip((upward(CHAIN), -upward(CHAIN), 4), outs):
        encode(*held(main_ref, (z + 8 + ahead) & 7), out_ref, 0)


def upward(by):
    return by - 2 * by * (lax.axis_index("z") & 1)


def step_kernel(ahead, main_ref, in_ref, *refs):
    out_ref = refs[-1]
    at = (lax.axis_index("z") + 8 + upward(ahead)) & 7
    encode(*added(held(main_ref, at), decode(in_ref, 0)), out_ref, 0)


def fold_kernel(main_ref, far_ref, out_ref):
    cells, weights = added(held(main_ref, lax.axis_index("z")), decode(far_ref, 0))
    for w in range(4):
        out_ref[0, w * TILE : (w + 1) * TILE, :] = cells[w]
    out_ref[0, 4 * TILE : 4 * TILE + 4, :] = weights


def finish_kernel(own_ref, *refs):
    ins, (coadd_ref, cover_ref) = refs[:-2], refs[-2:]
    cells, weights = added(held(own_ref, 0), *[decode(ref, 0) for ref in ins])
    lane = lax.broadcasted_iota(i32, (1, TILE), 1)
    cover = jnp.zeros((1, TILE), f32)
    for w in range(4):
        coadd_ref[0, w] = cells[w] / jnp.maximum(weights[w : w + 1], 1.0)
        cover = jnp.where(lane == w, weights[w : w + 1], cover)
    cover_ref[...] = cover[:, :4]


def local(images, psf_taps, exposure_weights, dest_patch, dest_cell, shift_class):
    shape = jax.ShapeDtypeStruct
    edge = (BAND - HALO) * (lax.axis_index("x") & 1)
    outer = lax.dynamic_slice_in_dim(images[0], edge, HALO)
    inner = lax.dynamic_slice_in_dim(images[0], BAND - HALO - edge, HALO)
    outer = lax.ppermute(outer, ("y", "x"), [p for i in range(1, 14, 2) for p in ((i, i + 1), (i + 1, i))])
    inner = lax.ppermute(inner, ("y", "x"), [p for i in range(0, 15, 2) for p in ((i, i + 1), (i + 1, i))])
    rows, cols = (jnp.asarray(t) for t in lanczos_tables())
    passed, info, over_cols, over_rows = call(
        columns_kernel,
        "columns",
        (
            shape((BAND, BLOCKS * TILE), bf16),
            shape((2,), i32),
            shape((2 * TILE, TILE), bf16),
            shape((2, FRAME, WINDOW), bf16),
        ),
        [HBM] * 4,
        (VMEM, SMEM, VMEM, VMEM),
        [
            pltpu.VMEM((2, KTAPS), bf16),
            pltpu.VMEM((2, COLS // TILE), i32),
            pltpu.VMEM((2, COLS // TILE), i32),
            pltpu.VMEM((BAND, COLS), bf16),
            pltpu.SemaphoreType.DMA((7,)),
        ],
    )(*(pltpu.with_memory_space_constraint(a, pltpu.HBM) for a in (psf_taps, dest_patch, dest_cell, images)))
    matched = call(
        rows_kernel,
        "rows",
        shape((2, FRAME, BLOCKS * TILE), bf16),
        [VMEM] * 5,
        VMEM,
        [pltpu.VMEM((BLOCKS * 2 * HALO, 2 * TILE), bf16), pltpu.VMEM((2 * HALO, BLOCKS * TILE), bf16)],
    )(over_cols, over_rows, inner, outer, passed)
    piece = shape((PIECE, TILE), bf16)
    own = [None] * 4
    sib = [None] * 4
    for sends in SENDS:
        outs = call(
            lambda *refs, sends=sends: warp_kernel(sends, *refs),
            f"warp_{len(sends)}",
            (piece,) * len(sends),
            [SMEM] * 4 + [VMEM] * 3,
            (VMEM,) * len(sends),
            [pltpu.VMEM((HALF_TILES * len(sends), FRAME, TILE), bf16)],
        )(info, dest_patch, shift_class, exposure_weights, rows, cols, matched)
        for (hop, swap), out in zip(sends, outs):
            if hop or swap:
                out = lax.ppermute(
                    out, ("core", "x"), [(c * 4 + i, (c ^ swap) * 4 + (i + hop) % 4) for c in range(2) for i in range(4)]
                )
            (sib if swap else own)[hop] = out
    held_rows = shape((8, CELLROW, TILE), f32)
    spill = shape((2 * CELLROW, TILE), i16)
    coded = shape((CELLROW, TILE), i16)
    spills = []
    for n, hops in enumerate(((1, 1, 3, 3), (0, 2, 2, 0))):
        out = call(
            lambda *refs, hops=hops: spill_kernel(hops, *refs),
            f"spill_{n}",
            spill,
            [VMEM] * 4,
            VMEM,
            [pltpu.VMEM((4, CELLROW, TILE), f32)],
        )(*(piece for hop in sorted(set(hops)) for piece in (own[hop], sib[hop])))
        lower = [(4 * i + x, 4 * i + 4 + x) for i in range(3) for x in range(4) if x % 2 == n]
        upper = [(4 * i + 4 + x, 4 * i + x) for i in range(3) for x in range(4) if x % 2 != n]
        spills.append(lax.ppermute(out, ("y", "x"), lower + upper))
    main = call(place_kernel, "place", held_rows, [VMEM] * 8, VMEM, [pltpu.VMEM((12, CELLROW, TILE), f32)])(*own, *sib)
    main, one, two, far = call(
        merge_kernel, "merge", (held_rows,) + (coded,) * 3, [VMEM] * 3, (VMEM,) * 4
    )(main, *spills)

    pairs = [[p for i in range(n, 8, 2) for p in ((i, (i + 1) % 8), ((i + 1) % 8, i))] for n in range(2)]
    far = lax.ppermute(far, "z", [(i, (i + 4) % 8) for i in range(8)])
    mine = call(fold_kernel, "fold", shape((1, CELLROW, TILE), f32), [VMEM] * 2, VMEM)(main, far)
    for s in range(CHAIN - 1, -1, -1):
        got_one, got_two = lax.ppermute(one, "z", pairs[0]), lax.ppermute(two, "z", pairs[1])
        one, two = got_two, got_one
        if s:
            after = (mine,) if s == LATE else ()
            ins = [VMEM] * (2 + len(after))
            one = call(lambda *refs, s=s: step_kernel(s, *refs), f"one_{s}", coded, ins, VMEM)(main, got_two, *after)
            two = call(lambda *refs, s=s: step_kernel(-s, *refs), f"two_{s}", coded, ins, VMEM)(main, got_one, *after)
    return call(
        finish_kernel,
        "finish",
        (shape((1, 4, TILE, TILE), f32), shape((1, 4), f32)),
        [VMEM] * 3,
        (VMEM, VMEM),
    )(mine, one, two)


def solution(mesh):
    split = Mesh(mesh.devices.reshape(8, 2, 4, 4), ("z", "core", "y", "x"))
    visit = ("z", "core")
    patch = ("y", "x")
    placed = (
        P(visit, patch, None),
        P(visit, None, None),
        P(visit),
        P(visit, patch, None),
        P(visit, patch, None),
        P(visit, None, patch, None),
    )
    return jax.shard_map(
        local,
        mesh=split,
        in_specs=placed,
        out_specs=(P(patch, visit, None, None), P(patch, visit)),
        check_vma=False,
    )
```

```python
import math

import jax
import jax.numpy as jnp
import numpy as np
from jax import lax
from jax.experimental import pallas as pl
from jax.experimental.pallas import tpu as pltpu
from jax.sharding import Mesh, PartitionSpec as P

TILE = 128
KTAPS = 13
SHIFTS = 8
HALO = 16
BAND = 256
COLS = 4096
BLOCKS = COLS // TILE + 1
EDGE = 122
FRAME = 144
WINDOW = FRAME + 16
LEAD = 119
HALF_TILES = 8
PIECE = HALF_TILES * TILE + 32
CELLROW = 4 * TILE + 16
TOP_CODE = 32000.0
SENDS = (((2, 0), (2, 1)), ((1, 0), (3, 0), (1, 1), (3, 1), (0, 0), (0, 1)))
LATE = 1
CHAIN = 3
f32 = jnp.float32
bf16 = jnp.bfloat16
i16 = jnp.int16
i32 = jnp.int32
SMEM = pl.BlockSpec(memory_space=pltpu.SMEM)
VMEM = pl.BlockSpec(memory_space=pltpu.VMEM)
HBM = pl.BlockSpec(memory_space=pltpu.HBM)


def call(kernel, name, out_shape, in_specs, out_specs, scratch=(), mib=8):
    return pl.pallas_call(
        kernel,
        out_shape=out_shape,
        in_specs=in_specs,
        out_specs=out_specs,
        scratch_shapes=scratch,
        compiler_params=pltpu.CompilerParams(vmem_limit_bytes=mib * 2**20),
        cost_estimate=pl.CostEstimate(flops=1, transcendentals=0, bytes_accessed=1),
        name=name,
    )


def lanczos_tables():
    out_pos = np.arange(TILE)[None, :, None]
    src_pos = np.arange(TILE + 6)[None, None, :] - 3.0
    frac = np.arange(SHIFTS)[:, None, None] / SHIFTS
    dist = src_pos - out_pos - frac
    kernel = np.where(np.abs(dist) < 3.0, np.sinc(dist) * np.sinc(dist / 3.0), 0.0)
    kernel = kernel / np.sum(kernel, axis=2, keepdims=True)
    along_rows = np.zeros((SHIFTS + 1, TILE, FRAME), np.float32)
    along_rows[:SHIFTS, :, : TILE + 6] = kernel
    along_cols = np.zeros((SHIFTS, 2 * TILE, TILE), np.float32)
    along_cols[:, LEAD : LEAD + TILE + 6] = kernel.transpose(0, 2, 1)
    return along_rows.astype(bf16), along_cols.astype(bf16)


def banded(taps, shape, base):
    diff = lax.broadcasted_iota(i32, shape, 0) - lax.broadcasted_iota(i32, shape, 1) + base
    total = jnp.zeros(shape, f32)
    for k in range(KTAPS):
        total = jnp.where(diff == k, taps[:, k : k + 1], total)
    return total


def columns_kernel(taps_hbm, patch_hbm, cell_hbm, img_hbm, out_ref, info_ref, cols_out, rows_out, taps_ref, patch_ref, cell_ref, img_ref, sems):
    small = [
        pltpu.make_async_copy(src.at[0], dst, sems.at[n])
        for n, (src, dst) in enumerate(((taps_hbm, taps_ref), (patch_hbm, patch_ref), (cell_hbm, cell_ref)))
    ]
    quarter = COLS // 4
    parts = []
    for n in range(4):
        at = slice(n * quarter, (n + 1) * quarter)
        parts.append(pltpu.make_async_copy(img_hbm.at[0, :, at], img_ref.at[:, at], sems.at[3 + n]))
    for copy in small + parts:
        copy.start()
    for copy in small:
        copy.wait()
    over_cols = banded(taps_ref[...].astype(f32)[1:2], (2 * TILE, TILE), 0)
    lane = lax.broadcasted_iota(i32, (TILE, TILE), 1)
    first = jnp.where(lane >= EDGE, over_cols[TILE:], 0.0).astype(bf16)
    last = jnp.where(lane < EDGE, over_cols[:TILE], 0.0).astype(bf16)
    over_cols = over_cols.astype(bf16)
    cols_out[...] = over_cols
    patch = lax.axis_index("y") * 4 + lax.axis_index("x")
    taps = taps_ref[...].astype(f32)
    shape = (FRAME, WINDOW)
    row = lax.broadcasted_iota(i32, shape, 0)
    base = jnp.zeros(shape, f32)
    step = lax.broadcasted_iota(i32, shape, 1) - row - 7
    for k in range(KTAPS):
        base = jnp.where(step == k, taps[0:1, k : k + 1], base)
    low = jnp.where(patch == 0, 3, 0)
    high = jnp.where(patch == 15, 130, 133)
    rows_out[0] = jnp.where((row >= low) & (row <= 133), base, 0.0).astype(bf16)
    rows_out[1] = jnp.where(row <= high, base, 0.0).astype(bf16)
    owner = patch_ref[...]
    cell = cell_ref[...]
    row0 = 2 * (lax.axis_index("y") * 4 + lax.axis_index("x"))
    down = (owner >> 2) * 8 + (cell >> 3) - lax.broadcasted_iota(i32, owner.shape, 0) - row0
    right = (owner & 3) * 8 + (cell & 7) - lax.broadcasted_iota(i32, owner.shape, 1)
    for n, offset in enumerate((down, right)):
        most = jnp.max(jnp.where(owner >= 0, offset.astype(f32), -8.0)).astype(i32)
        info_ref[n] = jnp.where(most > -8, jnp.clip(most, -2, 2), 0)
    for b in range(BLOCKS):
        if b % 8 == 0 and b < BLOCKS - 1:
            parts[b // 8].wait()
        if b == 0:
            window, weights = img_ref[:, :TILE], first
        elif b == BLOCKS - 1:
            window, weights = img_ref[:, COLS - TILE :], last
        else:
            window, weights = img_ref[:, (b - 1) * TILE : (b + 1) * TILE], over_cols
        out_ref[:, b * TILE : (b + 1) * TILE] = jnp.dot(window, weights, preferred_element_type=f32).astype(bf16)


def rows_kernel(cols_ref, rows_ref, inner_ref, outer_ref, passed_ref, out_ref, window_ref, edge_ref):
    patch = lax.axis_index("y") * 4 + lax.axis_index("x")
    over_cols = cols_ref[...]
    halo = 2 * HALO
    for odd, top_ref, bot_ref in ((0, outer_ref, inner_ref), (1, inner_ref, outer_ref)):

        @pl.when((patch & 1) == odd)
        def _(top_ref=top_ref, bot_ref=bot_ref):
            for b in range(BLOCKS):
                for side in range(2):
                    k = b - 1 + side
                    for n, ref in enumerate((top_ref, bot_ref)):
                        rows = jnp.zeros((HALO, TILE), bf16)
                        if 0 <= k < BLOCKS - 1:
                            rows = ref[:, k * TILE : (k + 1) * TILE]
                        first = b * halo + n * HALO
                        window_ref[first : first + HALO, side * TILE : (side + 1) * TILE] = rows

    lane = lax.broadcasted_iota(i32, (halo, TILE), 1)
    for part in range(3):
        each = BLOCKS // 3
        got = jnp.dot(
            window_ref[part * each * halo : (part + 1) * each * halo], over_cols, preferred_element_type=f32
        )
        for n in range(each):
            b = part * each + n
            rows = got[n * halo : (n + 1) * halo]
            if b == 0:
                rows = jnp.where(lane >= EDGE, rows, 0.0)
            if b == BLOCKS - 1:
                rows = jnp.where(lane < EDGE, rows, 0.0)
            edge_ref[:, b * TILE : (b + 1) * TILE] = rows.astype(bf16)
    for n in range(BLOCKS // 3):
        at = slice(n * 3 * TILE, (n + 1) * 3 * TILE)
        upper = jnp.concatenate([edge_ref[:HALO, at], passed_ref[:FRAME, at]], axis=0)
        lower = jnp.concatenate([passed_ref[BAND - FRAME :, at], edge_ref[HALO:, at]], axis=0)
        for r, window in enumerate((upper, lower)):
            out_ref[r, :, at] = jnp.dot(rows_ref[r], window, preferred_element_type=f32).astype(bf16)


def warp_kernel(sends, info_ref, patch_ref, class_ref, weight_ref, rows_ref, cols_ref, in_ref, *refs):
    out_refs, half_ref = refs[:-1], refs[-1]
    core = lax.axis_index("core")
    line = lax.broadcasted_iota(i32, (32, TILE), 0)
    weight = jnp.full((32, TILE), weight_ref[0], f32)
    high = weight.astype(bf16).astype(f32)
    mid = (weight - high).astype(bf16).astype(f32)
    low = weight - high - mid
    parts = jnp.where(line < 8, high, jnp.where(line < 16, mid, low))
    down = info_ref[0].astype(f32)
    plan = []
    for n, out_ref in enumerate(out_refs):
        dest = (lax.axis_index("x") + sends[n][0]) & 3
        half = 1 - core if sends[n][1] else core
        marks = jnp.zeros((32, TILE), f32)
        for slot in range(HALF_TILES):
            r, w = divmod(slot, 4)
            col = dest * 8 + half * 4 + w - info_ref[1]
            inside = (col >= 0) & (col < 32)
            col = jnp.clip(col, 0, 31)
            there = inside & (patch_ref[0, r, col] >= 0)
            plan.append((out_ref, slot, r, col, jnp.where(there, class_ref[0, 0, r, col], SHIFTS)))
            marks = jnp.where((line & 7) == slot, jnp.where(there, 1.0, 0.0), marks)
        out_ref[HALF_TILES * TILE :, :] = jnp.where(line < 24, marks * parts, down).astype(bf16)
    for n, (out_ref, slot, r, col, picked) in enumerate(plan):
        tile = in_ref[r, :, pl.ds(pl.multiple_of(col * TILE, TILE), 2 * TILE)]
        half_ref[n] = jnp.dot(tile, cols_ref[class_ref[0, 1, r, col]], preferred_element_type=f32).astype(bf16)
    for n, (out_ref, slot, r, col, picked) in enumerate(plan):
        out_ref[slot * TILE : (slot + 1) * TILE, :] = jnp.dot(
            rows_ref[picked], half_ref[n], preferred_element_type=f32
        ).astype(bf16)


def encode(cells, weights, out_ref, start):
    line = lax.broadcasted_iota(i32, (16, TILE), 0)
    notes = jnp.zeros((16, TILE), f32)
    for w in range(4):
        cell = cells[w]
        most = jnp.max(jnp.max(jnp.abs(cell), axis=0, keepdims=True), axis=1, keepdims=True)
        level = jnp.ceil(jnp.log(jnp.maximum(most, 1e-33)) * (128.0 / math.log(2.0)))
        code = jnp.floor(cell * (TOP_CODE * jnp.exp(level * (-math.log(2.0) / 128.0))) + 0.5)
        out_ref[start + w * TILE : start + (w + 1) * TILE, :] = code.astype(i32).astype(i16)
        whole = jnp.floor(weights[w : w + 1] * 128.0)
        rest = jnp.floor((weights[w : w + 1] * 128.0 - whole) * 32767.0 + 0.5)
        notes = jnp.where(line == w, level, notes)
        notes = jnp.where(line == 4 + w, whole, notes)
        notes = jnp.where(line == 8 + w, rest, notes)
    out_ref[start + 4 * TILE : start + CELLROW, :] = notes.astype(i32).astype(i16)


def decode(in_ref, start):
    notes = in_ref[start + 4 * TILE : start + CELLROW, :].astype(i32).astype(f32)
    cells = []
    for w in range(4):
        scale = jnp.exp(notes[w : w + 1] * (math.log(2.0) / 128.0)) * (1.0 / TOP_CODE)
        code = in_ref[start + w * TILE : start + (w + 1) * TILE, :].astype(i32).astype(f32)
        cells.append(code * scale)
    return cells, (notes[4:8] + notes[8:12] * (1.0 / 32767.0)) * (1.0 / 128.0)


def held(ref, at):
    cells = [ref[at, w * TILE : (w + 1) * TILE, :] for w in range(4)]
    return cells, ref[at, 4 * TILE : 4 * TILE + 4, :]


def added(*parts):
    cells = [sum(p[0][w] for p in parts[1:]) + parts[0][0][w] for w in range(4)]
    return cells, sum(p[1] for p in parts[1:]) + parts[0][1]


def spread(piece, rows_ref, where):
    notes = piece[HALF_TILES * TILE :, :].astype(f32)
    weights = notes[0:8] + notes[8:16] + notes[16:24]
    down = jnp.max(notes[24:32]).astype(i32)
    for r in range(2):
        at = where(r, r + down)
        for w in range(4):
            slot = r * 4 + w
            tile = piece[slot * TILE : (slot + 1) * TILE, :].astype(f32)
            rows_ref[at, w * TILE : (w + 1) * TILE, :] += weights[slot : slot + 1] * tile
        rows_ref[at, 4 * TILE : 4 * TILE + 4, :] += weights[r * 4 : r * 4 + 4]


def spill_kernel(hops, *refs):
    pieces, out_ref, rows_ref = refs[:4], refs[4], refs[5]
    x = lax.axis_index("x")
    rows_ref[...] = jnp.zeros(rows_ref.shape, f32)
    for n, hop in enumerate(sorted(set(hops))):
        mine = [i for i in range(4) if hops[i] == hop]
        band = (x + 4 - hop) & 3

        def where(r, row, band=band):
            slot = jnp.where(band == 0, row + 2, row - 2)
            return jnp.where((slot >= 0) & (slot < 2), slot, 2 + r)

        @pl.when((x == mine[0]) | (x == mine[1]))
        def _(n=n, where=where):
            for piece in pieces[n::2]:
                spread(piece, rows_ref, where)

    for r in range(2):
        encode(*held(rows_ref, r), out_ref, r * CELLROW)


def place_kernel(*refs):
    pieces, main_ref, rows_ref = refs[:8], refs[8], refs[9]
    rows_ref[...] = jnp.zeros(rows_ref.shape, f32)
    for n, piece in enumerate(pieces):
        band = (lax.axis_index("x") + 4 - n % 4) & 3
        spread(piece, rows_ref, lambda r, row: 2 * band + row + 2)
    main_ref[...] = rows_ref[2:10]


def merge_kernel(in_ref, *refs):
    spills, main_ref, outs = refs[:2], refs[2], refs[3:]
    main_ref[2:6] = in_ref[2:6]
    for n, ref in enumerate(spills):
        first = jnp.where((lax.axis_index("x") & 1) == n, 0, 6)
        for r in range(2):
            cells, weights = added(held(in_ref, first + r), decode(ref, r * CELLROW))
            for w in range(4):
                main_ref[first + r, w * TILE : (w + 1) * TILE, :] = cells[w]
            main_ref[first + r, 4 * TILE : 4 * TILE + 4, :] = weights
    z = lax.axis_index("z")
    for ahead, out_ref in zip((upward(CHAIN), -upward(CHAIN), 4), outs):
        encode(*held(main_ref, (z + 8 + ahead) & 7), out_ref, 0)


def upward(by):
    return by - 2 * by * (lax.axis_index("z") & 1)


def step_kernel(ahead, main_ref, in_ref, *refs):
    out_ref = refs[-1]
    at = (lax.axis_index("z") + 8 + upward(ahead)) & 7
    encode(*added(held(main_ref, at), decode(in_ref, 0)), out_ref, 0)


def fold_kernel(main_ref, far_ref, out_ref):
    cells, weights = added(held(main_ref, lax.axis_index("z")), decode(far_ref, 0))
    for w in range(4):
        out_ref[0, w * TILE : (w + 1) * TILE, :] = cells[w]
    out_ref[0, 4 * TILE : 4 * TILE + 4, :] = weights


def finish_kernel(own_ref, *refs):
    ins, (coadd_ref, cover_ref) = refs[:-2], refs[-2:]
    cells, weights = added(held(own_ref, 0), *[decode(ref, 0) for ref in ins])
    lane = lax.broadcasted_iota(i32, (1, TILE), 1)
    cover = jnp.zeros((1, TILE), f32)
    for w in range(4):
        coadd_ref[0, w] = cells[w] / jnp.maximum(weights[w : w + 1], 1.0)
        cover = jnp.where(lane == w, weights[w : w + 1], cover)
    cover_ref[...] = cover[:, :4]


def local(images, psf_taps, exposure_weights, dest_patch, dest_cell, shift_class):
    shape = jax.ShapeDtypeStruct
    edge = (BAND - HALO) * (lax.axis_index("x") & 1)
    outer = lax.dynamic_slice_in_dim(images[0], edge, HALO)
    inner = lax.dynamic_slice_in_dim(images[0], BAND - HALO - edge, HALO)
    outer = lax.ppermute(outer, ("y", "x"), [p for i in range(1, 14, 2) for p in ((i, i + 1), (i + 1, i))])
    inner = lax.ppermute(inner, ("y", "x"), [p for i in range(0, 15, 2) for p in ((i, i + 1), (i + 1, i))])
    rows, cols = (jnp.asarray(t) for t in lanczos_tables())
    passed, info, over_cols, over_rows = call(
        columns_kernel,
        "columns",
        (
            shape((BAND, BLOCKS * TILE), bf16),
            shape((2,), i32),
            shape((2 * TILE, TILE), bf16),
            shape((2, FRAME, WINDOW), bf16),
        ),
        [HBM] * 4,
        (VMEM, SMEM, VMEM, VMEM),
        [
            pltpu.VMEM((2, KTAPS), bf16),
            pltpu.VMEM((2, COLS // TILE), i32),
            pltpu.VMEM((2, COLS // TILE), i32),
            pltpu.VMEM((BAND, COLS), bf16),
            pltpu.SemaphoreType.DMA((7,)),
        ],
    )(*(pltpu.with_memory_space_constraint(a, pltpu.HBM) for a in (psf_taps, dest_patch, dest_cell, images)))
    matched = call(
        rows_kernel,
        "rows",
        shape((2, FRAME, BLOCKS * TILE), bf16),
        [VMEM] * 5,
        VMEM,
        [pltpu.VMEM((BLOCKS * 2 * HALO, 2 * TILE), bf16), pltpu.VMEM((2 * HALO, BLOCKS * TILE), bf16)],
    )(over_cols, over_rows, inner, outer, passed)
    piece = shape((PIECE, TILE), bf16)
    own = [None] * 4
    sib = [None] * 4
    for sends in SENDS:
        outs = call(
            lambda *refs, sends=sends: warp_kernel(sends, *refs),
            f"warp_{len(sends)}",
            (piece,) * len(sends),
            [SMEM] * 4 + [VMEM] * 3,
            (VMEM,) * len(sends),
            [pltpu.VMEM((HALF_TILES * len(sends), FRAME, TILE), bf16)],
        )(info, dest_patch, shift_class, exposure_weights, rows, cols, matched)
        for (hop, swap), out in zip(sends, outs):
            if hop or swap:
                out = lax.ppermute(
                    out, ("core", "x"), [(c * 4 + i, (c ^ swap) * 4 + (i + hop) % 4) for c in range(2) for i in range(4)]
                )
            (sib if swap else own)[hop] = out
    held_rows = shape((8, CELLROW, TILE), f32)
    spill = shape((2 * CELLROW, TILE), i16)
    coded = shape((CELLROW, TILE), i16)
    spills = []
    for n, hops in enumerate(((1, 1, 3, 3), (0, 2, 2, 0))):
        out = call(
            lambda *refs, hops=hops: spill_kernel(hops, *refs),
            f"spill_{n}",
            spill,
            [VMEM] * 4,
            VMEM,
            [pltpu.VMEM((4, CELLROW, TILE), f32)],
        )(*(piece for side in (sib, own) for piece in (side[hop] for hop in sorted(set(hops)))))
        lower = [(4 * i + x, 4 * i + 4 + x) for i in range(3) for x in range(4) if x % 2 == n]
        upper = [(4 * i + 4 + x, 4 * i + x) for i in range(3) for x in range(4) if x % 2 != n]
        spills.append(lax.ppermute(out, ("y", "x"), lower + upper))
    main = call(place_kernel, "place", held_rows, [VMEM] * 8, VMEM, [pltpu.VMEM((12, CELLROW, TILE), f32)])(*own, *sib)
    main, one, two, far = call(
        merge_kernel, "merge", (held_rows,) + (coded,) * 3, [VMEM] * 3, (VMEM,) * 4
    )(main, *spills)

    pairs = [[p for i in range(n, 8, 2) for p in ((i, (i + 1) % 8), ((i + 1) % 8, i))] for n in range(2)]
    far = lax.ppermute(far, "z", [(i, (i + 4) % 8) for i in range(8)])
    mine = call(fold_kernel, "fold", shape((1, CELLROW, TILE), f32), [VMEM] * 2, VMEM)(main, far)
    for s in range(CHAIN - 1, -1, -1):
        got_one, got_two = lax.ppermute(one, "z", pairs[0]), lax.ppermute(two, "z", pairs[1])
        one, two = got_two, got_one
        if s:
            after = (mine,) if s == LATE else ()
            ins = [VMEM] * (2 + len(after))
            one = call(lambda *refs, s=s: step_kernel(s, *refs), f"one_{s}", coded, ins, VMEM)(main, got_two, *after)
            two = call(lambda *refs, s=s: step_kernel(-s, *refs), f"two_{s}", coded, ins, VMEM)(main, got_one, *after)
    return call(
        finish_kernel,
        "finish",
        (shape((1, 4, TILE, TILE), f32), shape((1, 4), f32)),
        [VMEM] * 3,
        (VMEM, VMEM),
    )(mine, one, two)


def solution(mesh):
    split = Mesh(mesh.devices.reshape(8, 2, 4, 4), ("z", "core", "y", "x"))
    visit = ("z", "core")
    patch = ("y", "x")
    placed = (
        P(visit, patch, None),
        P(visit, None, None),
        P(visit),
        P(visit, patch, None),
        P(visit, patch, None),
        P(visit, None, patch, None),
    )
    return jax.shard_map(
        local,
        mesh=split,
        in_specs=placed,
        out_specs=(P(patch, visit, None, None), P(patch, visit)),
        check_vma=False,
    )
```
